256 devices in a mesh: dp: 32 (over z, x), passage: 8 (over y, core).
Axes of the slice: x: 4, y: 4, z: 8, core: 2. Of those that a mesh axis runs over, the one named last changes fastest.
Arguments:
- queries: bfloat16 [32, 256, 1024], P('dp'), may hold values from -300 to 300
- key_rows: bfloat16 [32, 4096, 1024], P('dp', 'passage'), may hold values from -20 to 20
- value_rows: bfloat16 [32, 4096, 1024], P('dp', 'passage'), may hold values from -6 to 6
- encoded: bfloat16 [32, 4096, 2048], P('dp', 'passage'), may hold values from -6 to 6
- key_weight: bfloat16 [2048, 1024], P('dp'), may hold values from -0.125 to 0.125
- value_weight: bfloat16 [2048, 1024], P('dp'), may hold values from -0.125 to 0.125
- grad_out: bfloat16 [32, 256, 1024], P('dp'), may hold values from -6 to 6
- lengths: int32 [32], P('dp'), may hold values from 64 to 256, as said below
Outputs:
- query_grad: bfloat16 [32, 256, 1024], P('dp', None, 'passage')
- encoded_grad: bfloat16 [32, 4096, 2048], P('dp', 'passage')
- key_weight_grad: float32 [2048, 1024], P(('dp', 'passage'))
- value_weight_grad: float32 [2048, 1024], P(('dp', 'passage'))
The draws below stay inside these ranges and needn't reach their ends.
Inputs may be any that keep to these rules, and one draw needn't show every extreme that they name: `lengths`: the first question's answer has all 256 tokens.
All inputs are finite; a program needn't handle non-finite values.
Results may differ from the reference program's by a relative error of at most 0.0065.
Values may be sent and summed in bfloat16 or wider, within the bound.
No kernel may reach another device: no remote copies, remote signals or barrier semaphores. Data moves between devices by JAX's collectives and lax.ppermute only.
A program may use at most 128 MiB of HBM per device.

```python
import math
import jax
import jax.numpy as jnp
from jax import lax

D = 2048
HEADS = 16
HEAD_DIM = 64
HD = 1024
ANS = 256
KEYS = 4096
QUESTIONS = 32


def draw_key_rows(key, part):
    key = jax.random.fold_in(key, 21)
    return jnp.clip(jax.random.normal(key, (QUESTIONS, KEYS, HD), jnp.float32), -6.0, 6.0).astype(jnp.bfloat16)


def draw_queries(key, part):
    own_key = jax.random.fold_in(key, 22)
    values = jnp.clip(jax.random.normal(own_key, (QUESTIONS, ANS, HD), jnp.float32), -6.0, 6.0)
    return values.astype(jnp.bfloat16)


def draw_lengths(key, part):
    key = jax.random.fold_in(key, 23)
    drawn = jax.random.randint(key, (QUESTIONS,), ANS // 4, ANS + 1, jnp.int32)
    return drawn.at[0].set(ANS)


def raised(entries, key, source, target, shards_of, factor):
    owner, partner = [(jnp.arange(entries.shape[position]) // (entries.shape[position] // shards_of)).reshape([-1 if axis == position else 1 for axis in range(entries.ndim)]) for position in (source, target)]
    chosen = jax.random.permutation(key, shards_of)[partner]
    strong = (owner == chosen) | (owner == (partner + shards_of // 2) % shards_of)
    return jnp.where(strong, factor * entries, entries)


def levels(key, extent, cuts, low, high):
    loudness, own = 1.0, jax.random.fold_in(key, 6)
    for dim, parts in cuts:
        draws = jnp.exp(jax.random.uniform(jax.random.fold_in(own, dim), (parts,), jnp.float32, low / len(cuts), high / len(cuts)))
        loudness = loudness * jnp.repeat(draws, extent[dim] // parts).reshape([-1 if axis == dim else 1 for axis in range(len(extent))])
    return loudness


def bell_draw(rng, extent, scale, limit, split=(), held_as=jnp.bfloat16):
    entries = jax.random.normal(rng, extent, jnp.float32) * scale
    if len(split) > 0:
        entries = levels(rng, extent, split, -0.22, 0.18) * entries
    return jnp.clip(entries, min=-limit, max=limit).astype(held_as)


def noise_with(rng, extent, scale, reach, shards, heavy, kind=jnp.bfloat16):
    values = scale * jax.random.normal(rng, extent, jnp.float32)
    if shards:
        values = values * levels(rng, extent, shards, -0.22, 0.18)
    return jnp.clip(raised(values, jax.random.fold_in(rng, 3), *heavy), -reach, reach).astype(kind)


def setup_inputs(seed: int = 0) -> dict:
    key_of = jax.random.split(jax.random.key(seed), 9)
    return {
        "queries": draw_queries(jax.random.fold_in(key_of[8], 71), 0),
        "key_rows": draw_key_rows(jax.random.fold_in(key_of[8], 71), 0),
        "value_rows": bell_draw(key_of[2], (QUESTIONS, KEYS, HD), 1.0, 6.0, ((0, 32), (1, 8))),
        "encoded": noise_with(key_of[3], (QUESTIONS, KEYS, D), 1.0, 6.0, ((0, 32), (1, 8)), (1, 2, 8, 2.0)),
        "key_weight": bell_draw(key_of[4], (D, HD), D ** -0.5, 0.125, ((0, 32),)),
        "value_weight": bell_draw(key_of[5], (D, HD), D ** -0.5, 0.125, ((0, 32),)),
        "grad_out": bell_draw(key_of[6], (QUESTIONS, ANS, HD), 1.0, 6.0, ((0, 32),)),
        "lengths": draw_lengths(jax.random.fold_in(key_of[8], 71), 0),
    }


def one_question(query_rows, key_part, value_part, encoder_rows, cotangent, length, key_weight, value_weight):
    answer = query_rows.shape[0]
    score_scale = 1.0 / math.sqrt(HEAD_DIM)
    live_rows = (jnp.arange(answer) < length).astype(jnp.bfloat16)
    masked = cotangent * live_rows[:, None]
    query_heads = query_rows.reshape(answer, HEADS, HEAD_DIM).astype(jnp.float32)
    key_heads = key_part.reshape(-1, HEADS, HEAD_DIM).astype(jnp.float32)
    value_heads = value_part.reshape(-1, HEADS, HEAD_DIM).astype(jnp.float32)
    grad_heads = masked.reshape(answer, HEADS, HEAD_DIM).astype(jnp.float32)
    scores = jnp.einsum('ihe,jhe->hij', query_heads, key_heads) * score_scale
    peak = lax.optimization_barrier(jnp.max(scores, axis=-1, keepdims=True))
    expo = jnp.exp(scores - peak)
    prob = expo / lax.optimization_barrier(jnp.sum(expo, axis=-1, keepdims=True))
    prob_grad = jnp.einsum('ihe,jhe->hij', grad_heads, value_heads)
    row_delta = lax.optimization_barrier(jnp.sum(prob * prob_grad, axis=-1, keepdims=True))
    prob_low = prob.astype(jnp.bfloat16)
    score_grad = (prob * (prob_grad - row_delta) * score_scale).astype(jnp.bfloat16)
    query_grad = jnp.einsum('hij,jhe->ihe', score_grad.astype(jnp.float32), key_heads)
    query_grad = query_grad.reshape(answer, HD).astype(jnp.bfloat16)
    key_grad = jnp.einsum('hij,ihe->jhe', score_grad.astype(jnp.float32), query_heads).reshape(-1, HD).astype(jnp.bfloat16)
    value_grad = jnp.einsum('hij,ihe->jhe', prob_low.astype(jnp.float32), grad_heads).reshape(-1, HD).astype(jnp.bfloat16)
    encoded_grad = jnp.dot(key_grad, key_weight.T, preferred_element_type=jnp.float32)
    encoded_grad = encoded_grad + jnp.dot(value_grad, value_weight.T, preferred_element_type=jnp.float32)
    joined = jnp.concatenate([key_grad, value_grad], axis=1)
    weight_term = jnp.dot(encoder_rows.T, joined, preferred_element_type=jnp.float32)
    return (query_grad, encoded_grad.astype(jnp.bfloat16), weight_term)

def reference(queries, key_rows, value_rows, encoded, key_weight, value_weight, grad_out, lengths):

    def step(carry, items):
        query_rows, key_part, value_part, encoder_rows, cotangent, length = items
        query_grad, encoded_grad, weight_term = one_question(query_rows, key_part, value_part, encoder_rows, cotangent, length, key_weight, value_weight)
        return (carry + weight_term, (query_grad, encoded_grad))
    start = jnp.zeros((D, 2 * HD), jnp.float32)
    total, outputs = lax.scan(step, start, (queries, key_rows, value_rows, encoded, grad_out, lengths))
    return (outputs[0], outputs[1], total[:, :HD], total[:, HD:])
```

```python
import functools
import math

import jax
import jax.numpy as jnp
from jax import lax
from jax.experimental import pallas as pl
from jax.experimental.pallas import tpu as pltpu
from jax.sharding import PartitionSpec as P

HEADS = 16
HEAD_DIM = 64
PAIR = 2 * HEAD_DIM
SCALE = 1.0 / math.sqrt(HEAD_DIM)
EXP2_SCALE = SCALE * math.log2(math.e)
NZ, NX, NY, NC = 8, 4, 4, 2
AXES = ("dp", "passage")
VMEM_LIMIT = 40 * 1024 * 1024


def device_index(z, x, y, c):
    return ((z % NZ) * NX + x % NX) * (NY * NC) + (y % NY) * NC + c % NC


def permutation(target):
    return [
        (device_index(z, x, y, c), device_index(*target(z, x, y, c)))
        for z in range(NZ)
        for x in range(NX)
        for y in range(NY)
        for c in range(NC)
    ]


def groups(key):
    found = {}
    for z in range(NZ):
        for x in range(NX):
            for y in range(NY):
                for c in range(NC):
                    found.setdefault(key(z, x, y, c), []).append(device_index(z, x, y, c))
    return list(found.values())


def swap_cores(value):
    return lax.ppermute(value, AXES, permutation(lambda z, x, y, c: (z, x, y, 1 - c)))


def two_heads(rows):
    lane = lax.broadcasted_iota(jnp.int32, rows.shape, 1)
    wide = rows.astype(jnp.float32)
    first = jnp.where(lane < HEAD_DIM, wide, 0.0)
    second = jnp.where(lane < HEAD_DIM, 0.0, wide)
    return jnp.concatenate([first, second], axis=0).astype(jnp.bfloat16)


def live_grads(length_ref, grad_ref):
    rows = grad_ref[...].astype(jnp.float32)
    position = lax.broadcasted_iota(jnp.int32, rows.shape, 0)
    return two_heads(jnp.where(position < length_ref[0], rows, 0.0))


def dot_last(left, right):
    return lax.dot_general(left, right, (((1,), (1,)), ((), ())), preferred_element_type=jnp.float32)


def stats_kernel(length_ref, query_ref, key_ref, value_ref, grad_ref, out_ref):
    pair = pl.program_id(0)
    scores = dot_last(key_ref[...], two_heads(query_ref[...]))
    prob_grad = dot_last(value_ref[...], live_grads(length_ref, grad_ref))
    peak = jnp.max(scores, axis=0, keepdims=True)
    expo = jnp.exp2((scores - peak) * EXP2_SCALE)
    out_ref[pl.ds(pair, 1), :] = peak
    out_ref[pl.ds(8 + pair, 1), :] = jnp.sum(expo, axis=0, keepdims=True)
    out_ref[pl.ds(16 + pair, 1), :] = jnp.sum(expo * prob_grad, axis=0, keepdims=True)


def grads_kernel(
    length_ref, query_ref, key_ref, value_ref, grad_ref, stats_ref, key_grad_ref, value_grad_ref, query_grad_ref
):
    pair = pl.program_id(0)
    peaks = stats_ref[:, pl.ds(pair, 1), :]
    sums = stats_ref[:, pl.ds(8 + pair, 1), :]
    deltas = stats_ref[:, pl.ds(16 + pair, 1), :]
    peak = jnp.max(peaks, axis=0)
    weight = jnp.exp2((peaks - peak[None]) * EXP2_SCALE)
    total = jnp.sum(sums * weight, axis=0)
    row_delta = jnp.sum(deltas * weight, axis=0) / total
    inverse = 1.0 / total
    key = key_ref[...]
    queries = two_heads(query_ref[...])
    grads = live_grads(length_ref, grad_ref)
    scores = dot_last(key, queries)
    prob_grad = dot_last(value_ref[...], grads)
    prob = jnp.exp2((scores - peak) * EXP2_SCALE) * inverse
    prob_low = prob.astype(jnp.bfloat16)
    score_grad = (prob * (prob_grad - row_delta)).astype(jnp.bfloat16)
    value_grad = jnp.dot(prob_low, grads, preferred_element_type=jnp.float32)
    key_grad = jnp.dot(score_grad, queries, preferred_element_type=jnp.float32)
    key_grad_ref[...] = (key_grad * SCALE).astype(jnp.bfloat16)
    value_grad_ref[...] = value_grad.astype(jnp.bfloat16)
    flipped = key.T
    answer = queries.shape[0] // 2
    query_grad_ref[:HEAD_DIM, :] = SCALE * jnp.dot(
        flipped[:HEAD_DIM], score_grad[:, :answer], preferred_element_type=jnp.float32
    )
    query_grad_ref[HEAD_DIM:, :] = SCALE * jnp.dot(
        flipped[HEAD_DIM:], score_grad[:, answer:], preferred_element_type=jnp.float32
    )


def transpose_kernel(in_ref, out_ref):
    out_ref[...] = in_ref[...].T


def weights_kernel(place_ref, own_ref, other_ref, grad_own_ref, grad_other_ref, *refs):
    outs, total = refs[:-1], refs[-1]
    total[...] = jnp.dot(own_ref[...], grad_own_ref[...], preferred_element_type=jnp.float32) + jnp.dot(
        other_ref[...], grad_other_ref[...], preferred_element_type=jnp.float32
    )
    half = total.shape[1] // 2
    for step in range(NX):
        chosen = lax.rem(place_ref[0] + step, NX)
        rows = total[pl.ds(pl.multiple_of(chosen * 64, 64), 64), :half]
        outs[step][0] = rows.astype(outs[step].dtype)
    for step in range(NY):
        chosen = lax.rem(place_ref[1] + step, NY)
        for x in range(NX):
            rows = total[pl.ds(pl.multiple_of(x * 64 + chosen * 16, 16), 16), half:]
            outs[NX + step][0, x] = rows.astype(outs[NX + step].dtype)


def encoded_kernel(key_ref, value_ref, weight_ref, out_ref):
    half = key_ref.shape[1]
    total = dot_last(key_ref[...], weight_ref[:, :half]) + dot_last(value_ref[...], weight_ref[:, half:])
    out_ref[...] = total.astype(jnp.bfloat16)


def params():
    return pltpu.CompilerParams(vmem_limit_bytes=VMEM_LIMIT)


def cost(flops, moved, exps=0):
    return pl.CostEstimate(flops=flops, bytes_accessed=moved, transcendentals=exps)


def on_device(queries, key_rows, value_rows, encoded, key_weight, value_weight, grad_out, lengths):
    _, answer, features = queries.shape
    keys = key_rows.shape[1]
    width = encoded.shape[2]
    pairs = features // PAIR
    dp, passage = lax.axis_index("dp"), lax.axis_index("passage")
    core = passage % NC
    queries, grad_out = queries[0], grad_out[0]
    key_rows, value_rows, encoded = key_rows[0], value_rows[0], encoded[0]

    weights = lax.all_gather(jnp.concatenate([key_weight, value_weight], axis=1), "dp", axis=0, tiled=True)

    smem = pl.BlockSpec(memory_space=pltpu.SMEM)
    row_spec = pl.BlockSpec((answer, PAIR), lambda p: (0, p))
    key_spec = pl.BlockSpec((keys, PAIR), lambda p: (0, p))
    stats = pl.pallas_call(
        stats_kernel,
        grid=(pairs,),
        in_specs=[smem, row_spec, key_spec, key_spec, row_spec],
        out_specs=pl.BlockSpec((3 * pairs, 2 * answer), lambda p: (0, 0)),
        out_shape=jax.ShapeDtypeStruct((3 * pairs, 2 * answer), jnp.float32),
        compiler_params=params(),
        cost_estimate=cost(4 * answer * keys * features, 4 * 2**20, answer * keys * HEADS),
        name="stats",
    )(lengths, queries, key_rows, value_rows, grad_out)
    others = [
        lax.ppermute(stats, AXES, permutation(lambda z, x, y, c: (z, x, y + dy, c + dc)))
        for dy in range(NY)
        for dc in range(NC)
        if dy or dc
    ]

    flipped = pl.pallas_call(
        transpose_kernel,
        grid=(width // 256,),
        in_specs=[pl.BlockSpec((keys, 256), lambda i: (0, i))],
        out_specs=pl.BlockSpec((256, keys), lambda i: (i, 0)),
        out_shape=jax.ShapeDtypeStruct((width, keys), jnp.bfloat16),
        compiler_params=params(),
        cost_estimate=cost(0, 4 * 2**20),
        name="flip",
    )(encoded)
    flipped_other = swap_cores(flipped)

    all_stats = jnp.stack([stats, *others])
    key_grad, value_grad, query_terms = pl.pallas_call(
        grads_kernel,
        grid=(pairs,),
        in_specs=[
            smem,
            row_spec,
            key_spec,
            key_spec,
            row_spec,
            pl.BlockSpec(all_stats.shape, lambda p: (0, 0, 0)),
        ],
        out_specs=[key_spec, key_spec, pl.BlockSpec((PAIR, answer), lambda p: (p, 0))],
        out_shape=[
            jax.ShapeDtypeStruct((keys, features), jnp.bfloat16),
            jax.ShapeDtypeStruct((keys, features), jnp.bfloat16),
            jax.ShapeDtypeStruct((features, answer), jnp.float32),
        ],
        compiler_params=params(),
        cost_estimate=cost(10 * answer * keys * features, 8 * 2**20, answer * keys * HEADS),
        name="grads",
    )(lengths, queries, key_rows, value_rows, grad_out, all_stats)

    query_grad = lax.psum_scatter(query_terms, "passage", scatter_dimension=0, tiled=True)
    query_grad = query_grad.T.astype(jnp.bfloat16)[None]

    first = core == 0
    mine = jnp.where(first, key_grad, value_grad)
    received = swap_cores(jnp.where(first, value_grad, key_grad))
    place = jnp.stack([dp % NX, passage // NC]).astype(jnp.int32)
    half = features // 2
    x_shape, y_shape = (NZ, 64, half), (NZ, NX, 16, half)
    x_spec = pl.BlockSpec((1, 64, half), lambda i: (i, 0, 0))
    y_spec = pl.BlockSpec((1, NX, 16, half), lambda i: (i, 0, 0, 0))
    whole = pl.BlockSpec((keys, features), lambda i: (0, 0))
    rows = pl.BlockSpec((width // NZ, keys), lambda i: (i, 0))
    kinds = [jnp.float32] + [jnp.bfloat16] * 3
    terms = pl.pallas_call(
        weights_kernel,
        grid=(NZ,),
        in_specs=[smem, rows, rows, whole, whole],
        out_specs=[x_spec] * NX + [y_spec] * NY,
        out_shape=[jax.ShapeDtypeStruct(x_shape, kind) for kind in kinds]
        + [jax.ShapeDtypeStruct(y_shape, kind) for kind in kinds],
        scratch_shapes=[pltpu.VMEM((width // NZ, features), jnp.float32)],
        compiler_params=params(),
        cost_estimate=cost(4 * keys * width * features, 12 * 2**20),
        name="weights",
    )(place, flipped, flipped_other, mine, received)
    x_terms, y_terms = terms[:NX], terms[NX:]
    x_got = [
        lax.ppermute(x_terms[k], AXES, permutation(lambda z, x, y, c: (z, x + k, y, c))) for k in range(1, NX)
    ]
    y_got = [
        lax.ppermute(y_terms[k], AXES, permutation(lambda z, x, y, c: (z, x, y + k, c))) for k in range(1, NY)
    ]
    x_sum = x_terms[0] + sum(t.astype(jnp.float32) for t in x_got)
    y_sum = y_terms[0] + sum(t.astype(jnp.float32) for t in y_got)
    x_sum = x_sum.astype(jnp.bfloat16).reshape(NZ * NY * NC, 8, half)
    y_sum = y_sum.astype(jnp.bfloat16).reshape(NZ * NX * NC, 8, half)
    x_all = lax.all_to_all(
        x_sum, AXES, 0, 0, tiled=True, axis_index_groups=groups(lambda z, x, y, c: x)
    )
    y_all = lax.all_to_all(
        y_sum, AXES, 0, 0, tiled=True, axis_index_groups=groups(lambda z, x, y, c: y)
    )
    x_all = x_all.reshape(NZ * NY, NC, 8, half).astype(jnp.float32).sum(0)
    y_all = y_all.reshape(NZ * NX, NC, 8, half).astype(jnp.float32).sum(0)
    summed = jnp.concatenate([x_all, y_all], axis=2)

    encoded_grad = pl.pallas_call(
        encoded_kernel,
        grid=(width // 256,),
        in_specs=[
            pl.BlockSpec((keys, features), lambda i: (0, 0)),
            pl.BlockSpec((keys, features), lambda i: (0, 0)),
            pl.BlockSpec((256, 2 * features), lambda i: (i, 0)),
        ],
        out_specs=pl.BlockSpec((keys, 256), lambda i: (0, i)),
        out_shape=jax.ShapeDtypeStruct((keys, width), jnp.bfloat16),
        compiler_params=params(),
        cost_estimate=cost(4 * keys * width * features, 12 * 2**20),
        name="encoded",
    )(key_grad, value_grad, weights)
    return query_grad, encoded_grad[None], summed[0], summed[1]


def solution(mesh):
    return jax.shard_map(
        on_device,
        mesh=mesh,
        in_specs=(
            P("dp", None, None),
            P("dp", "passage", None),
            P("dp", "passage", None),
            P("dp", "passage", None),
            P("dp", None),
            P("dp", None),
            P("dp", None, None),
            P("dp"),
        ),
        out_specs=(
            P("dp", None, "passage"),
            P("dp", "passage", None),
            P(("dp", "passage"), None),
            P(("dp", "passage"), None),
        ),
        check_vma=False,
    )
```

```python
import functools
import math

import jax
import jax.numpy as jnp
from jax import lax
from jax.experimental import pallas as pl
from jax.experimental.pallas import tpu as pltpu
from jax.sharding import PartitionSpec as P

HEADS = 16
HEAD_DIM = 64
PAIR = 2 * HEAD_DIM
SCALE = 1.0 / math.sqrt(HEAD_DIM)
EXP2_SCALE = SCALE * math.log2(math.e)
NZ, NX, NY, NC = 8, 4, 4, 2
AXES = ("dp", "passage")
MIB = 1024 * 1024


def device_index(z, x, y, c):
    return ((z % NZ) * NX + x % NX) * (NY * NC) + (y % NY) * NC + c % NC


def permutation(target):
    return [
        (device_index(z, x, y, c), device_index(*target(z, x, y, c)))
        for z in range(NZ)
        for x in range(NX)
        for y in range(NY)
        for c in range(NC)
    ]


def groups(key):
    found = {}
    for z in range(NZ):
        for x in range(NX):
            for y in range(NY):
                for c in range(NC):
                    found.setdefault(key(z, x, y, c), []).append(device_index(z, x, y, c))
    return list(found.values())


def swap_cores(value):
    return lax.ppermute(value, AXES, permutation(lambda z, x, y, c: (z, x, y, 1 - c)))


def two_heads(rows):
    lane = lax.broadcasted_iota(jnp.int32, rows.shape, 1)
    wide = rows.astype(jnp.float32)
    first = jnp.where(lane < HEAD_DIM, wide, 0.0)
    second = jnp.where(lane < HEAD_DIM, 0.0, wide)
    return jnp.concatenate([first, second], axis=0).astype(jnp.bfloat16)


def live_grads(length_ref, grad):
    rows = grad.astype(jnp.float32)
    position = lax.broadcasted_iota(jnp.int32, rows.shape, 0)
    return two_heads(jnp.where(position < length_ref[0], rows, 0.0))


def dot_last(left, right):
    return lax.dot_general(left, right, (((1,), (1,)), ((), ())), preferred_element_type=jnp.float32)


def merged(rows, pairs):
    peak = jnp.max(rows[:, :pairs], axis=0)
    weight = jnp.exp2((rows[:, :pairs] - peak[None]) * EXP2_SCALE)
    total = jnp.sum(rows[:, pairs : 2 * pairs] * weight, axis=0)
    delta = jnp.sum(rows[:, 2 * pairs :] * weight, axis=0)
    return peak, total, delta


def stats_kernel(length_ref, query_ref, key_ref, value_ref, grad_ref, out_ref):
    for part in range(2):
        lanes = slice(part * PAIR, part * PAIR + PAIR)
        pair = 2 * pl.program_id(0) + part
        scores = dot_last(key_ref[:, lanes], two_heads(query_ref[:, lanes]))
        prob_grad = dot_last(value_ref[:, lanes], live_grads(length_ref, grad_ref[:, lanes]))
        peak = jnp.max(scores, axis=0, keepdims=True)
        expo = jnp.exp2((scores - peak) * EXP2_SCALE)
        out_ref[pl.ds(pair, 1), :] = peak
        out_ref[pl.ds(8 + pair, 1), :] = jnp.sum(expo, axis=0, keepdims=True)
        out_ref[pl.ds(16 + pair, 1), :] = jnp.sum(expo * prob_grad, axis=0, keepdims=True)


def merge_kernel(left_ref, right_ref, out_ref):
    pairs = out_ref.shape[0] // 3
    peak, total, delta = merged(jnp.stack([left_ref[...], right_ref[...]]), pairs)
    out_ref[:pairs] = peak
    out_ref[pairs : 2 * pairs] = total
    out_ref[2 * pairs :] = delta


def grads_kernel(first_pair, core_ref, length_ref, query_ref, key_ref, value_ref, grad_ref, *refs):
    stats_refs = refs[:NY]
    mine_ref, sent_ref, query_kept_ref, query_sent_ref = refs[NY:]
    keeps_key = core_ref[0] == 0
    query_grads = []
    for part in range(2):
        lanes = slice(part * PAIR, part * PAIR + PAIR)
        pair = first_pair + 2 * pl.program_id(0) + part
        rows = jnp.stack([
            jnp.concatenate([ref[pl.ds(start + pair, 1), :] for start in (0, 8, 16)], axis=0)
            for ref in stats_refs
        ])
        peak, total, delta = merged(rows, 1)
        row_delta = delta / total
        inverse = 1.0 / total
        key = key_ref[:, lanes]
        queries = two_heads(query_ref[:, lanes])
        grads = live_grads(length_ref, grad_ref[:, lanes])
        scores = dot_last(key, queries)
        prob_grad = dot_last(value_ref[:, lanes], grads)
        prob = jnp.exp2((scores - peak) * EXP2_SCALE) * inverse
        prob_low = prob.astype(jnp.bfloat16)
        score_grad = (prob * (prob_grad - row_delta)).astype(jnp.bfloat16)
        value_grad = jnp.dot(prob_low, grads, preferred_element_type=jnp.float32)
        key_grad = jnp.dot(score_grad, queries, preferred_element_type=jnp.float32) * SCALE
        mine_ref[:, lanes] = jnp.where(keeps_key, key_grad, value_grad).astype(jnp.bfloat16)
        sent_ref[:, lanes] = jnp.where(keeps_key, value_grad, key_grad).astype(jnp.bfloat16)
        flipped = key.T
        answer = queries.shape[0] // 2
        query_grads.append(
            SCALE
            * jnp.concatenate(
                [
                    jnp.dot(flipped[:HEAD_DIM], score_grad[:, :answer], preferred_element_type=jnp.float32),
                    jnp.dot(flipped[HEAD_DIM:], score_grad[:, answer:], preferred_element_type=jnp.float32),
                ],
                axis=0,
            )
        )
    even, odd = query_grads
    query_kept_ref[0] = jnp.where(keeps_key, even, odd)
    query_sent_ref[0] = jnp.where(keeps_key, odd, even).astype(jnp.bfloat16)


def arrange_kernel(place_ref, *refs):
    shards, out_ref = refs[:-1], refs[-1]
    rows = shards[0].shape[0]
    for k, shard in enumerate(shards):
        first = lax.rem(place_ref[0] + NX - k, NX) * rows
        out_ref[pl.ds(pl.multiple_of(first, rows), rows), :] = shard[...]


def split(place_ref, first, rows_of, refs):
    kept_left, sent_left, kept_right, sent_right = refs
    for kept, sent, near, far, side in ((kept_left, sent_left, 1, 3, 0), (kept_right, sent_right, 3, 1, 1)):
        for out, order in ((kept, (0, far)), (sent, (near, 2))):
            for index, flip in enumerate(order):
                rows_of(out.at[index], place_ref[first + flip], side)


def side_of(ref, index, rows, side):
    half = ref.shape[-1] // 2
    return ref[index, rows, side * half : side * half + half]


def weights_kernel(place_ref, own_ref, other_ref, *refs):
    own_grads, other_grads, query_refs = refs[:2], refs[2:4], refs[4:8]
    x_outs, y_outs = refs[8:12], refs[12:16]
    x_total, y_total, query_total = refs[16:]
    own, other = own_ref[...].T, other_ref[...].T
    for total, own_grad, other_grad in zip((x_total, y_total), own_grads, other_grads):
        total[0] = jnp.dot(own, own_grad[...], preferred_element_type=jnp.float32) + jnp.dot(
            other, other_grad[...], preferred_element_type=jnp.float32
        )
    for y in range(NY):
        kept, received = query_refs[y // 2], query_refs[2 + y // 2]
        for side in range(2):
            first = pl.multiple_of(side * 64 + pl.program_id(0) * 16, 16)
            rows = kept[y % 2, pl.ds(first, 16), :] + received[y % 2, pl.ds(first, 16), :].astype(jnp.float32)
            query_total[y, side] = rows

    def x_rows(out, chosen, side):
        for z in range(out.shape[0]):
            rows = pl.ds(pl.multiple_of(z * 256 + chosen * 64, 64), 64)
            out[z] = side_of(x_total, 0, rows, side).astype(out.dtype)

    def y_rows(out, chosen, side):
        for z in range(NZ // 4):
            for x in range(NX):
                rows = pl.ds(pl.multiple_of(z * 256 + x * 64 + chosen * 16, 16), 16)
                row = (z * NX + x) * 16
                out[0, row : row + 16] = side_of(y_total, 0, rows, side).astype(out.dtype)
        out[0, NZ // 4 * NX * 16 :] = query_total[chosen, side].astype(out.dtype)

    split(place_ref, 0, x_rows, x_outs)
    split(place_ref, 4, y_rows, y_outs)


def middle_kernel(*refs):
    parts = len(refs) // 3
    for kept, received, out in zip(refs[:parts], refs[parts : 2 * parts], refs[2 * parts :]):
        out[...] = (kept[0] + received[0].astype(jnp.float32)).astype(out.dtype)


def add_parts(refs, total):
    half = total.shape[-1] // 2
    for side in range(2):
        kept, first, last = refs[side], refs[2 + side], refs[4 + side]
        rows = kept[0] + first[0].astype(jnp.float32) + last[...].astype(jnp.float32)
        total[:, :, side * half : side * half + half] = rows


def second_kernel(place_ref, *refs):
    add_parts(refs[:6], refs[-2])
    add_parts(refs[6:12], refs[-1])
    x_outs, y_outs = refs[12:16], refs[16:20]
    query_out, x_total, y_total = refs[20:]
    query_out[...] = y_total[:, NZ // 4 * NX * 16 :]

    def x_rows(out, chosen, side):
        for z in range(NZ // 4):
            rows = pl.ds(pl.multiple_of(chosen * 16, 16), 16)
            out[z] = side_of(x_total, z, rows, side).astype(out.dtype)

    def y_rows(out, chosen, side):
        for z in range(NZ // 4):
            rows = pl.ds(pl.multiple_of(z * NX * 16 + chosen * 16, 16), 16)
            out[z] = side_of(y_total, 0, rows, side).astype(out.dtype)

    split(place_ref, 4, x_rows, x_outs)
    split(place_ref, 0, y_rows, y_outs)


def last_kernel(*refs):
    out, x_total, y_total = refs[12:]
    half = x_total.shape[2]
    add_parts(refs[:6], x_total)
    add_parts(refs[6:12], y_total)
    out[:, :, :half] = x_total[...].astype(out.dtype)
    out[:, :, half:] = y_total[...].astype(out.dtype)


def encoded_kernel(*refs):
    grads, weights, out_ref = refs[:4], refs[4:-1], refs[-1]
    half = grads[0].shape[1]
    total = None
    for index, grad in enumerate(grads):
        part = index % 2
        term = dot_last(grad[...], weights[index // 2][:, part * half : part * half + half])
        total = term if total is None else total + term
    out_ref[...] = total.astype(jnp.bfloat16)


def kernel_call(kernel, name, out_shape, mebibytes=24, flops=0, moved=0, **options):
    return pl.pallas_call(
        kernel,
        out_shape=out_shape,
        compiler_params=pltpu.CompilerParams(vmem_limit_bytes=mebibytes * MIB),
        cost_estimate=pl.CostEstimate(flops=flops, bytes_accessed=moved, transcendentals=0),
        name=name,
        **options,
    )


def like(shape, dtype):
    return jax.ShapeDtypeStruct(shape, dtype)


def along(axis, step):
    def target(z, x, y, c):
        return (
            z + step * (axis == "z"),
            x + step * (axis == "x"),
            y + step * (axis == "y"),
            c + step * (axis == "core"),
        )

    return permutation(target)


def send(value, links):
    return lax.ppermute(value, AXES, links)


def tie(value, *after):
    return lax.optimization_barrier((value, *after))[0]


def flipped(axis, bits):
    return permutation(lambda z, x, y, c: (z, x ^ bits if axis == "x" else x, y ^ bits if axis == "y" else y, c))


def halving(outs, axes, steps):
    kept, sent = outs[0::2], outs[1::2]
    ways = [(axis, *bits) for axis in axes for bits in ((1, 3), (3, 1))]
    first = [send(value, flipped(axis, near)) for value, (axis, near, _) in zip(sent, ways)]
    first = lax.optimization_barrier(first)

    def block(shape):
        return pl.BlockSpec((1, shape[1] // steps, *shape[2:]), lambda i: (1, i, 0, 0))

    shapes = [value.shape for value in kept]
    middle = kernel_call(
        middle_kernel,
        "middle",
        [like(shape[1:], jnp.bfloat16) for shape in shapes],
        grid=(steps,),
        in_specs=[block(shape) for shape in shapes] * 2,
        out_specs=[pl.BlockSpec((shape[1] // steps, *shape[2:]), lambda i: (i, 0, 0)) for shape in shapes],
    )(*kept, *first)
    last = [send(value, flipped(axis, far)) for value, (axis, _, far) in zip(middle, ways)]
    last = lax.optimization_barrier(last)
    operands, specs = [], []
    for start in (0, 2):
        for values in (kept, first, last):
            for value in values[start : start + 2]:
                operands.append(value)
                inner = value.shape[-3:]
                shape = (1,) * (value.ndim - 3) + (inner[0] // steps, *inner[1:])
                leading = (0,) * (value.ndim - 3)
                specs.append(pl.BlockSpec(shape, lambda i, leading=leading: (*leading, i, 0, 0)))
    return operands, specs


def on_device(queries, key_rows, value_rows, encoded, key_weight, value_weight, grad_out, lengths):
    _, answer, features = queries.shape
    keys = key_rows.shape[1]
    width = encoded.shape[2]
    pairs = features // PAIR
    half = features // 2
    dp, passage = lax.axis_index("dp").astype(jnp.int32), lax.axis_index("passage").astype(jnp.int32)
    x_place, y_place, core = dp % NX, passage // NC, passage % NC
    place = jnp.stack([p ^ bits for p in (x_place, y_place) for bits in range(4)])
    queries, grad_out = queries[0], grad_out[0]
    key_rows, value_rows, encoded = key_rows[0], value_rows[0], encoded[0]
    f32, bf16 = jnp.float32, jnp.bfloat16
    encoded_other = swap_cores(encoded)
    smem = pl.BlockSpec(memory_space=pltpu.SMEM)

    shard = jnp.where(core == 0, key_weight, value_weight)
    shards = [shard] + [send(shard, along("x", k)) for k in range(1, NX)]

    stats_shape = like((3 * pairs, 2 * answer), f32)
    row_spec = pl.BlockSpec((answer, 2 * PAIR), lambda p: (0, p))
    key_spec = pl.BlockSpec((keys, 2 * PAIR), lambda p: (0, p))
    stats = kernel_call(
        stats_kernel,
        "stats",
        stats_shape,
        62,
        grid=(pairs // 2,),
        in_specs=[smem, row_spec, key_spec, key_spec, row_spec],
        out_specs=pl.BlockSpec(stats_shape.shape, lambda p: (0, 0)),
    )(lengths, queries, key_rows, value_rows, grad_out)

    whole_vmem = pl.BlockSpec(memory_space=pltpu.VMEM)
    shards = lax.optimization_barrier((*shards, stats))[:-1]
    ordered = kernel_call(
        arrange_kernel,
        "arrange",
        like((NX * shard.shape[0], features), bf16),
        in_specs=[smem] + [whole_vmem] * NX,
        out_specs=whole_vmem,
    )(place, *shards)
    gathered = lax.all_gather(
        ordered, AXES, axis=0, tiled=True, axis_index_groups=groups(lambda z, x, y, c: (x, y, c))
    )

    chip_stats = kernel_call(merge_kernel, "merge", stats_shape)(tie(stats, ordered), swap_cores(stats))
    all_stats = [chip_stats] + [send(chip_stats, along("y", k)) for k in range(1, NY)]

    def grads(first_pair):
        def rows(p):
            return (0, first_pair // 2 + p)

        row_spec = pl.BlockSpec((answer, 2 * PAIR), rows)
        key_spec = pl.BlockSpec((keys, 2 * PAIR), rows)
        out_spec = pl.BlockSpec((keys, 2 * PAIR), lambda p: (0, p))
        stats_spec = pl.BlockSpec(stats_shape.shape, lambda p: (0, 0))
        query_spec = pl.BlockSpec((1, PAIR, answer), lambda p: (p, 0, 0))
        return kernel_call(
            functools.partial(grads_kernel, first_pair),
            "grads",
            [
                like((keys, half), bf16),
                like((keys, half), bf16),
                like((NY // 2, PAIR, answer), f32),
                like((NY // 2, PAIR, answer), bf16),
            ],
            grid=(pairs // 4,),
            in_specs=[smem, smem, row_spec, key_spec, key_spec, row_spec] + [stats_spec] * NY,
            out_specs=[out_spec, out_spec, query_spec, query_spec],
        )(core[None], lengths, queries, key_rows, value_rows, grad_out, *all_stats)

    mine_a, sent_a, query_kept_a, query_sent_a = grads(0)
    received_a = swap_cores(sent_a)
    mine_b, sent_b, query_kept_b, query_sent_b = grads(pairs // 2)
    received_b = swap_cores(sent_b)
    query_received = [swap_cores(query_sent_a), swap_cores(query_sent_b)]

    def blocks(shape):
        return pl.BlockSpec((shape[0] // 4, *shape[1:]), lambda i: (i, 0, 0))

    whole = pl.BlockSpec((keys, half), lambda i: (0, 0))
    encoded_spec = pl.BlockSpec((keys, width // 4), lambda i: (0, i))
    query_spec = pl.BlockSpec(query_kept_a.shape, lambda i: (0, 0, 0))
    query_rows = PAIR * answer // half // 4
    x_shape = (2, NZ, 64, half // 2)
    y_shape = (2, 4, NZ // 4 * NX * 16 + query_rows, half // 2)

    def split_outs(shape):
        spec = pl.BlockSpec((2, shape[1] // 4, *shape[2:]), lambda i: (0, i, 0, 0))
        return [like(shape, f32), like(shape, bf16)] * 2, [spec] * 4

    def total(shape):
        return pltpu.VMEM((shape[1] // 4, shape[2], 2 * shape[3]), f32)

    x_outs, x_specs = split_outs(x_shape)
    y_outs, y_specs = split_outs(y_shape)
    terms = kernel_call(
        weights_kernel,
        "weights",
        x_outs + y_outs,
        grid=(4,),
        in_specs=[smem, encoded_spec, encoded_spec] + [whole] * 4 + [query_spec] * 4,
        out_specs=x_specs + y_specs,
        scratch_shapes=[pltpu.VMEM((1, width // 4, half), f32)] * 2
        + [pltpu.VMEM((NY, 2, query_rows, answer), f32)],
    )(
        place,
        encoded,
        encoded_other,
        mine_a,
        mine_b,
        received_a,
        received_b,
        query_kept_a,
        query_kept_b,
        *query_received,
    )

    operands, specs = halving(terms, "xy", 4)
    chunk, query_shape = (2, NZ, 16, half // 2), (4, query_rows, half)
    chunk_outs, chunk_specs = split_outs(chunk)
    *second, query_grad = kernel_call(
        second_kernel,
        "second",
        chunk_outs * 2 + [like(query_shape, f32)],
        grid=(4,),
        in_specs=[smem] + specs,
        out_specs=chunk_specs * 2 + [blocks(query_shape)],
        scratch_shapes=[total(x_shape), total(y_shape)],
    )(place, *operands)
    query_grad = query_grad.reshape(4, query_rows, 2, answer).transpose(2, 0, 1, 3)
    query_grad = query_grad.reshape(PAIR, answer).T.astype(bf16)[None]

    operands, specs = halving(second, "yx", 1)
    last = kernel_call(
        last_kernel,
        "last",
        like((NZ, 16, features), bf16),
        grid=(1,),
        in_specs=specs,
        out_specs=pl.BlockSpec((NZ, 16, features), lambda i: (0, 0, 0)),
        scratch_shapes=[pltpu.VMEM((NZ, 16, half), f32)] * 2,
    )(*operands)
    gathered = tie(gathered, last)
    gathered_other = swap_cores(gathered)
    last = lax.all_to_all(
        last.reshape(NZ * NC, 8, features),
        AXES,
        0,
        0,
        tiled=True,
        axis_index_groups=groups(lambda z, x, y, c: (x, y)),
    )

    weight_spec = pl.BlockSpec((width // 4, features), lambda i: (i, 0))
    encoded_grad = kernel_call(
        encoded_kernel,
        "encoded",
        like((keys, width), bf16),
        flops=4 * keys * width * features,
        moved=14 * MIB,
        grid=(4,),
        in_specs=[whole] * 4 + [weight_spec] * 2,
        out_specs=pl.BlockSpec((keys, width // 4), lambda i: (0, i)),
    )(mine_a, mine_b, sent_a, sent_b, gathered, gathered_other)
    summed = tie(last, encoded_grad).reshape(NZ, NC, 8, features).astype(f32).sum(0)
    key_weight_grad, value_weight_grad = summed[0], summed[1]
    return query_grad, encoded_grad[None], key_weight_grad, value_weight_grad


def solution(mesh):
    return jax.shard_map(
        on_device,
        mesh=mesh,
        in_specs=(
            P("dp", None, None),
            P("dp", "passage", None),
            P("dp", "passage", None),
            P("dp", "passage", None),
            P("dp", None),
            P("dp", None),
            P("dp", None, None),
            P("dp"),
        ),
        out_specs=(
            P("dp", None, "passage"),
            P("dp", "passage", None),
            P(("dp", "passage"), None),
            P(("dp", "passage"), None),
        ),
        check_vma=False,
    )
```

```python
import functools
import math

import jax
import jax.numpy as jnp
from jax import lax
from jax.experimental import pallas as pl
from jax.experimental.pallas import tpu as pltpu
from jax.sharding import PartitionSpec as P

HEADS = 16
HEAD_DIM = 64
PAIR = 2 * HEAD_DIM
SCALE = 1.0 / math.sqrt(HEAD_DIM)
EXP2_SCALE = SCALE * math.log2(math.e)
NZ, NX, NY, NC = 8, 4, 4, 2
AXES = ("dp", "passage")
MIB = 1024 * 1024


def device_index(z, x, y, c):
    return ((z % NZ) * NX + x % NX) * (NY * NC) + (y % NY) * NC + c % NC


def permutation(target):
    return [
        (device_index(z, x, y, c), device_index(*target(z, x, y, c)))
        for z in range(NZ)
        for x in range(NX)
        for y in range(NY)
        for c in range(NC)
    ]


def groups(key):
    found = {}
    for z in range(NZ):
        for x in range(NX):
            for y in range(NY):
                for c in range(NC):
                    found.setdefault(key(z, x, y, c), []).append(device_index(z, x, y, c))
    return list(found.values())


def swap_cores(value):
    return lax.ppermute(value, AXES, permutation(lambda z, x, y, c: (z, x, y, 1 - c)))


def two_heads(rows):
    lane = lax.broadcasted_iota(jnp.int32, rows.shape, 1)
    wide = rows.astype(jnp.float32)
    first = jnp.where(lane < HEAD_DIM, wide, 0.0)
    second = jnp.where(lane < HEAD_DIM, 0.0, wide)
    return jnp.concatenate([first, second], axis=0).astype(jnp.bfloat16)


def live_grads(length_ref, grad):
    rows = grad.astype(jnp.float32)
    position = lax.broadcasted_iota(jnp.int32, rows.shape, 0)
    return two_heads(jnp.where(position < length_ref[0], rows, 0.0))


def dot_last(left, right):
    return lax.dot_general(left, right, (((1,), (1,)), ((), ())), preferred_element_type=jnp.float32)


def merged(rows, pairs):
    peak = jnp.max(rows[:, :pairs], axis=0)
    weight = jnp.exp2((rows[:, :pairs] - peak[None]) * EXP2_SCALE)
    total = jnp.sum(rows[:, pairs : 2 * pairs] * weight, axis=0)
    delta = jnp.sum(rows[:, 2 * pairs :] * weight, axis=0)
    return peak, total, delta


def stats_kernel(length_ref, query_ref, key_ref, value_ref, grad_ref, out_ref):
    for part in range(2):
        lanes = slice(part * PAIR, part * PAIR + PAIR)
        pair = 2 * pl.program_id(0) + part
        scores = dot_last(key_ref[:, lanes], two_heads(query_ref[:, lanes]))
        prob_grad = dot_last(value_ref[:, lanes], live_grads(length_ref, grad_ref[:, lanes]))
        peak = jnp.max(scores, axis=0, keepdims=True)
        expo = jnp.exp2((scores - peak) * EXP2_SCALE)
        out_ref[pl.ds(pair, 1), :] = peak
        out_ref[pl.ds(8 + pair, 1), :] = jnp.sum(expo, axis=0, keepdims=True)
        out_ref[pl.ds(16 + pair, 1), :] = jnp.sum(expo * prob_grad, axis=0, keepdims=True)


def merge_kernel(left_ref, right_ref, out_ref):
    pairs = out_ref.shape[0] // 3
    peak, total, delta = merged(jnp.stack([left_ref[...], right_ref[...]]), pairs)
    out_ref[:pairs] = peak
    out_ref[pairs : 2 * pairs] = total
    out_ref[2 * pairs :] = delta


def grads_kernel(first_pair, core_ref, length_ref, query_ref, key_ref, value_ref, grad_ref, *refs):
    stats_refs = refs[:NY]
    mine_ref, sent_ref, query_kept_ref, query_sent_ref = refs[NY:]
    keeps_key = core_ref[0] == 0
    query_grads = []
    for part in range(2):
        lanes = slice(part * PAIR, part * PAIR + PAIR)
        pair = first_pair + 2 * pl.program_id(0) + part
        rows = jnp.stack([
            jnp.concatenate([ref[pl.ds(start + pair, 1), :] for start in (0, 8, 16)], axis=0)
            for ref in stats_refs
        ])
        peak, total, delta = merged(rows, 1)
        row_delta = delta / total
        inverse = 1.0 / total
        key = key_ref[:, lanes]
        queries = two_heads(query_ref[:, lanes])
        grads = live_grads(length_ref, grad_ref[:, lanes])
        scores = dot_last(key, queries)
        prob_grad = dot_last(value_ref[:, lanes], grads)
        prob = jnp.exp2((scores - peak) * EXP2_SCALE) * inverse
        prob_low = prob.astype(jnp.bfloat16)
        score_grad = (prob * (prob_grad - row_delta)).astype(jnp.bfloat16)
        value_grad = jnp.dot(prob_low, grads, preferred_element_type=jnp.float32)
        key_grad = jnp.dot(score_grad, queries, preferred_element_type=jnp.float32) * SCALE
        mine_ref[:, lanes] = jnp.where(keeps_key, key_grad, value_grad).astype(jnp.bfloat16)
        sent_ref[:, lanes] = jnp.where(keeps_key, value_grad, key_grad).astype(jnp.bfloat16)
        flipped = key.T
        answer = queries.shape[0] // 2
        query_grads.append(
            SCALE
            * jnp.concatenate(
                [
                    jnp.dot(flipped[:HEAD_DIM], score_grad[:, :answer], preferred_element_type=jnp.float32),
                    jnp.dot(flipped[HEAD_DIM:], score_grad[:, answer:], preferred_element_type=jnp.float32),
                ],
                axis=0,
            )
        )
    even, odd = query_grads
    query_kept_ref[0] = jnp.where(keeps_key, even, odd)
    query_sent_ref[0] = jnp.where(keeps_key, odd, even).astype(jnp.bfloat16)


def arrange_kernel(place_ref, *refs):
    shards, out_ref = refs[:-1], refs[-1]
    rows = shards[0].shape[1]
    for k, shard in enumerate(shards):
        first = lax.rem(place_ref[0] + NX - k, NX) * rows
        out_ref[:, pl.ds(pl.multiple_of(first, rows), rows), :] = shard[...]


def split(place_ref, first, rows_of, refs):
    kept_left, sent_left, kept_right, sent_right = refs
    for kept, sent, near, far, side in ((kept_left, sent_left, 1, 3, 0), (kept_right, sent_right, 3, 1, 1)):
        for out, order in ((kept, (0, far)), (sent, (near, 2))):
            for index, flip in enumerate(order):
                rows_of(out.at[index], place_ref[first + flip], side)


def side_of(ref, index, rows, side):
    half = ref.shape[-1] // 2
    return ref[index, rows, side * half : side * half + half]


def weights_kernel(place_ref, own_ref, other_ref, *refs):
    own_grads, other_grads, query_refs = refs[:2], refs[2:4], refs[4:8]
    x_outs, y_outs = refs[8:12], refs[12:16]
    x_total, y_total, query_total = refs[16:]
    own, other = own_ref[...].T, other_ref[...].T
    for total, own_grad, other_grad in zip((x_total, y_total), own_grads, other_grads):
        total[0] = jnp.dot(own, own_grad[...], preferred_element_type=jnp.float32) + jnp.dot(
            other, other_grad[...], preferred_element_type=jnp.float32
        )
    for y in range(NY):
        kept, received = query_refs[y // 2], query_refs[2 + y // 2]
        for side in range(2):
            first = pl.multiple_of(side * 64 + pl.program_id(0) * 16, 16)
            rows = kept[y % 2, pl.ds(first, 16), :] + received[y % 2, pl.ds(first, 16), :].astype(jnp.float32)
            query_total[y, side] = rows

    def x_rows(out, chosen, side):
        for z in range(out.shape[0]):
            rows = pl.ds(pl.multiple_of(z * 256 + chosen * 64, 64), 64)
            out[z] = side_of(x_total, 0, rows, side).astype(out.dtype)

    def y_rows(out, chosen, side):
        for z in range(NZ // 4):
            for x in range(NX):
                rows = pl.ds(pl.multiple_of(z * 256 + x * 64 + chosen * 16, 16), 16)
                row = (z * NX + x) * 16
                out[0, row : row + 16] = side_of(y_total, 0, rows, side).astype(out.dtype)
        out[0, NZ // 4 * NX * 16 :] = query_total[chosen, side].astype(out.dtype)

    split(place_ref, 0, x_rows, x_outs)
    split(place_ref, 4, y_rows, y_outs)


def middle_kernel(*refs):
    parts = len(refs) // 3
    for kept, received, out in zip(refs[:parts], refs[parts : 2 * parts], refs[2 * parts :]):
        out[...] = (kept[0] + received[0].astype(jnp.float32)).astype(out.dtype)


def add_parts(refs, total):
    half = total.shape[-1] // 2
    for side in range(2):
        kept, first, last = refs[side], refs[2 + side], refs[4 + side]
        rows = kept[0] + first[0].astype(jnp.float32) + last[...].astype(jnp.float32)
        total[:, :, side * half : side * half + half] = rows


def second_kernel(place_ref, *refs):
    add_parts(refs[:6], refs[-2])
    add_parts(refs[6:12], refs[-1])
    x_outs, y_outs = refs[12:16], refs[16:20]
    query_out, x_total, y_total = refs[20:]
    query_out[...] = y_total[:, NZ // 4 * NX * 16 :]

    def x_rows(out, chosen, side):
        for z in range(NZ // 4):
            rows = pl.ds(pl.multiple_of(chosen * 16, 16), 16)
            out[z] = side_of(x_total, z, rows, side).astype(out.dtype)

    def y_rows(out, chosen, side):
        for z in range(NZ // 4):
            rows = pl.ds(pl.multiple_of(z * NX * 16 + chosen * 16, 16), 16)
            out[z] = side_of(y_total, 0, rows, side).astype(out.dtype)

    split(place_ref, 4, x_rows, x_outs)
    split(place_ref, 0, y_rows, y_outs)


def last_kernel(*refs):
    out, x_total, y_total = refs[12:]
    half = x_total.shape[2]
    add_parts(refs[:6], x_total)
    add_parts(refs[6:12], y_total)
    out[:, :, :half] = x_total[...].astype(out.dtype)
    out[:, :, half:] = y_total[...].astype(out.dtype)


def encoded_kernel(order_ref, *refs):
    grads, pieces, out_ref, results, sems = refs[:4], refs[4:-3], *refs[-3:]
    half = grads[0].shape[1]
    core = order_ref[NZ]
    stores = []
    for k, piece in enumerate(pieces):
        total = None
        for index, grad in enumerate(grads):
            side, part = lax.rem(core + index // 2, NC), index % 2
            term = dot_last(grad[...], piece[side, :, part * half : part * half + half])
            total = term if total is None else total + term
        results[k] = total.astype(jnp.bfloat16)
        columns = pl.ds(pl.multiple_of(order_ref[k] * 256, 256), 256)
        store = pltpu.make_async_copy(results.at[k], out_ref.at[:, columns], sems.at[k])
        store.start()
        stores.append(store)
    for store in stores:
        store.wait()


def kernel_call(kernel, name, out_shape, mebibytes=12, flops=0, moved=0, **options):
    return pl.pallas_call(
        kernel,
        out_shape=out_shape,
        compiler_params=pltpu.CompilerParams(vmem_limit_bytes=mebibytes * MIB),
        cost_estimate=pl.CostEstimate(flops=flops, bytes_accessed=moved, transcendentals=0),
        name=name,
        **options,
    )


def like(shape, dtype):
    return jax.ShapeDtypeStruct(shape, dtype)


def along(axis, step):
    def target(z, x, y, c):
        return (
            z + step * (axis == "z"),
            x + step * (axis == "x"),
            y + step * (axis == "y"),
            c + step * (axis == "core"),
        )

    return permutation(target)


def send(value, links):
    return lax.ppermute(value, AXES, links)


def tie(value, *after):
    return lax.optimization_barrier((value, *after))[0]


def flipped(axis, bits):
    return permutation(lambda z, x, y, c: (z, x ^ bits if axis == "x" else x, y ^ bits if axis == "y" else y, c))


def halving(outs, axes, steps, beside=()):
    kept, sent = outs[0::2], outs[1::2]
    ways = [(axis, *bits) for axis in axes for bits in ((1, 3), (3, 1))]
    first = [send(value, flipped(axis, near)) for value, (axis, near, _) in zip(sent, ways)]
    first = lax.optimization_barrier(first)

    def block(shape):
        return pl.BlockSpec((1, shape[1] // steps, *shape[2:]), lambda i: (1, i, 0, 0))

    shapes = [value.shape for value in kept]
    middle = kernel_call(
        middle_kernel,
        "middle",
        [like(shape[1:], jnp.bfloat16) for shape in shapes],
        grid=(steps,),
        in_specs=[block(shape) for shape in shapes] * 2,
        out_specs=[pl.BlockSpec((shape[1] // steps, *shape[2:]), lambda i: (i, 0, 0)) for shape in shapes],
    )(*kept, *first)
    last = [send(value, flipped(axis, far)) for value, (axis, _, far) in zip(middle, ways)]
    last, beside = lax.optimization_barrier((last, beside))
    operands, specs = [], []
    for start in (0, 2):
        for values in (kept, first, last):
            for value in values[start : start + 2]:
                operands.append(value)
                inner = value.shape[-3:]
                shape = (1,) * (value.ndim - 3) + (inner[0] // steps, *inner[1:])
                leading = (0,) * (value.ndim - 3)
                specs.append(pl.BlockSpec(shape, lambda i, leading=leading: (*leading, i, 0, 0)))
    return operands, specs, middle[0], beside


def on_device(queries, key_rows, value_rows, encoded, key_weight, value_weight, grad_out, lengths):
    _, answer, features = queries.shape
    keys = key_rows.shape[1]
    width = encoded.shape[2]
    pairs = features // PAIR
    half = features // 2
    dp, passage = lax.axis_index("dp").astype(jnp.int32), lax.axis_index("passage").astype(jnp.int32)
    x_place, y_place, core = dp % NX, passage // NC, passage % NC
    place = jnp.stack([p ^ bits for p in (x_place, y_place) for bits in range(4)])
    queries, grad_out = queries[0], grad_out[0]
    key_rows, value_rows, encoded = key_rows[0], value_rows[0], encoded[0]
    f32, bf16 = jnp.float32, jnp.bfloat16
    smem = pl.BlockSpec(memory_space=pltpu.SMEM)

    shard = jnp.stack([key_weight, value_weight])
    shards = [shard] + [send(shard, along("x", k)) for k in range(1, NX)]

    stats_shape = like((3 * pairs, 2 * answer), f32)
    row_spec = pl.BlockSpec((answer, 2 * PAIR), lambda p: (0, p))
    key_spec = pl.BlockSpec((keys, 2 * PAIR), lambda p: (0, p))
    stats = kernel_call(
        stats_kernel,
        "stats",
        stats_shape,
        62,
        grid=(pairs // 2,),
        in_specs=[smem, row_spec, key_spec, key_spec, row_spec],
        out_specs=pl.BlockSpec(stats_shape.shape, lambda p: (0, 0)),
    )(lengths, queries, key_rows, value_rows, grad_out)

    chip_stats = kernel_call(merge_kernel, "merge", stats_shape)(stats, swap_cores(stats))
    all_stats = [chip_stats] + [send(chip_stats, along("y", k)) for k in (1, 3)]
    *shards, encoded_other, late = lax.optimization_barrier((*shards, swap_cores(encoded), chip_stats))
    all_stats.append(send(late, along("y", 2)))

    def grads(first_pair):
        def rows(p):
            return (0, first_pair // 2 + p)

        row_spec = pl.BlockSpec((answer, 2 * PAIR), rows)
        key_spec = pl.BlockSpec((keys, 2 * PAIR), rows)
        out_spec = pl.BlockSpec((keys, 2 * PAIR), lambda p: (0, p))
        stats_spec = pl.BlockSpec(stats_shape.shape, lambda p: (0, 0))
        query_spec = pl.BlockSpec((1, PAIR, answer), lambda p: (p, 0, 0))
        return kernel_call(
            functools.partial(grads_kernel, first_pair),
            "grads",
            [
                like((keys, half), bf16),
                pltpu.HBM((keys, half), bf16),
                like((NY // 2, PAIR, answer), f32),
                like((NY // 2, PAIR, answer), bf16),
            ],
            grid=(pairs // 4,),
            in_specs=[smem, smem, row_spec, key_spec, key_spec, row_spec] + [stats_spec] * NY,
            out_specs=[out_spec, out_spec, query_spec, query_spec],
        )(core[None], lengths, queries, key_rows, value_rows, grad_out, *all_stats)

    mine_a, sent_a, query_kept_a, query_sent_a = grads(0)
    received_a = swap_cores(sent_a)

    whole_vmem = pl.BlockSpec(memory_space=pltpu.VMEM)
    shards = lax.optimization_barrier((*shards, mine_a))[:-1]
    ordered = kernel_call(
        arrange_kernel,
        "arrange",
        like((2, NX * shard.shape[1], features), bf16),
        in_specs=[smem] + [whole_vmem] * NX,
        out_specs=whole_vmem,
    )(place, *shards)

    around = permutation(lambda z, x, y, c: (z + 1 - 2 * c, x, y, c))
    pieces = [ordered, send(ordered, around)]

    mine_b, sent_b, query_kept_b, query_sent_b = grads(pairs // 2)
    received_b = swap_cores(sent_b)
    query_received = [swap_cores(query_sent_a), swap_cores(query_sent_b)]

    def blocks(shape):
        return pl.BlockSpec((shape[0] // 4, *shape[1:]), lambda i: (i, 0, 0))

    whole = pl.BlockSpec((keys, half), lambda i: (0, 0))
    encoded_spec = pl.BlockSpec((keys, width // 4), lambda i: (0, i))
    query_spec = pl.BlockSpec(query_kept_a.shape, lambda i: (0, 0, 0))
    query_rows = PAIR * answer // half // 4
    x_shape = (2, NZ, 64, half // 2)
    y_shape = (2, 4, NZ // 4 * NX * 16 + query_rows, half // 2)

    def split_outs(shape):
        spec = pl.BlockSpec((2, shape[1] // 4, *shape[2:]), lambda i: (0, i, 0, 0))
        return [like(shape, f32), like(shape, bf16)] * 2, [spec] * 4

    def total(shape):
        return pltpu.VMEM((shape[1] // 4, shape[2], 2 * shape[3]), f32)

    x_outs, x_specs = split_outs(x_shape)
    y_outs, y_specs = split_outs(y_shape)
    terms = kernel_call(
        weights_kernel,
        "weights",
        x_outs + y_outs,
        20,
        grid=(4,),
        in_specs=[smem, encoded_spec, encoded_spec] + [whole] * 4 + [query_spec] * 4,
        out_specs=x_specs + y_specs,
        scratch_shapes=[pltpu.VMEM((1, width // 4, half), f32)] * 2
        + [pltpu.VMEM((NY, 2, query_rows, answer), f32)],
    )(
        place,
        encoded,
        encoded_other,
        mine_a,
        mine_b,
        received_a,
        received_b,
        query_kept_a,
        query_kept_b,
        *query_received,
    )

    pieces.append(send(tie(pieces[1], terms[0]), around))

    operands, specs, middle, _ = halving(terms, "xy", 4)
    pieces.append(send(tie(pieces[2], middle), around))
    chunk, query_shape = (2, NZ, 16, half // 2), (4, query_rows, half)
    chunk_outs, chunk_specs = split_outs(chunk)
    *second, query_grad = kernel_call(
        second_kernel,
        "second",
        chunk_outs * 2 + [like(query_shape, f32)],
        grid=(4,),
        in_specs=[smem] + specs,
        out_specs=chunk_specs * 2 + [blocks(query_shape)],
        scratch_shapes=[total(x_shape), total(y_shape)],
    )(place, *operands)
    query_grad = query_grad.reshape(4, query_rows, 2, answer).transpose(2, 0, 1, 3)
    query_grad = query_grad.reshape(PAIR, answer).T.astype(bf16)[None]

    across = send(tie(pieces[3], second[0]), around)
    operands, specs, _, across = halving(second, "yx", 1, across)
    last = kernel_call(
        last_kernel,
        "last",
        like((NZ, 16, features), bf16),
        grid=(1,),
        in_specs=specs,
        out_specs=pl.BlockSpec((NZ, 16, features), lambda i: (0, 0, 0)),
        scratch_shapes=[pltpu.VMEM((NZ, 16, half), f32)] * 2,
    )(*operands)
    swapped = [swap_cores(tie(piece, last)) for piece in pieces[1:4]]
    last = lax.all_to_all(
        last.reshape(NZ * NC, 8, features),
        AXES,
        0,
        0,
        tiled=True,
        axis_index_groups=groups(lambda z, x, y, c: (x, y)),
    )

    z_place, way = dp // NX, 1 - 2 * core
    order = [(z_place + way * step + NZ) % NZ for step in (0, -1, -2, -3, 1, 2, 3, 4)]
    in_hbm = pl.BlockSpec(memory_space=pltpu.HBM)
    encoded_grad = kernel_call(
        encoded_kernel,
        "encoded",
        pltpu.HBM((keys, width), bf16),
        24,
        flops=4 * keys * width * features,
        moved=14 * MIB,
        in_specs=[smem] + [whole_vmem] * (NZ + 4),
        out_specs=in_hbm,
        scratch_shapes=[
            pltpu.VMEM((NZ, keys, width // NZ), bf16),
            pltpu.SemaphoreType.DMA((NZ,)),
        ],
    )(jnp.stack([*order, core]), mine_a, mine_b, sent_a, sent_b, *pieces, *swapped, across)
    summed = tie(last, encoded_grad).reshape(NZ, NC, 8, features).astype(f32).sum(0)
    key_weight_grad, value_weight_grad = summed[0], summed[1]
    return query_grad, encoded_grad[None], key_weight_grad, value_weight_grad


def solution(mesh):
    return jax.shard_map(
        on_device,
        mesh=mesh,
        in_specs=(
            P("dp", None, None),
            P("dp", "passage", None),
            P("dp", "passage", None),
            P("dp", "passage", None),
            P("dp", None),
            P("dp", None),
            P("dp", None, None),
            P("dp"),
        ),
        out_specs=(
            P("dp", None, "passage"),
            P("dp", "passage", None),
            P(("dp", "passage"), None),
            P(("dp", "passage"), None),
        ),
        check_vma=False,
    )
```

```python
import functools
import math

import jax
import jax.numpy as jnp
from jax import lax
from jax.experimental import pallas as pl
from jax.experimental.pallas import tpu as pltpu
from jax.sharding import PartitionSpec as P

HEADS = 16
HEAD_DIM = 64
PAIR = 2 * HEAD_DIM
SCALE = 1.0 / math.sqrt(HEAD_DIM)
EXP2_SCALE = SCALE * math.log2(math.e)
NZ, NX, NY, NC = 8, 4, 4, 2
AXES = ("dp", "passage")
MIB = 1024 * 1024


def device_index(z, x, y, c):
    return ((z % NZ) * NX + x % NX) * (NY * NC) + (y % NY) * NC + c % NC


def permutation(target):
    return [
        (device_index(z, x, y, c), device_index(*target(z, x, y, c)))
        for z in range(NZ)
        for x in range(NX)
        for y in range(NY)
        for c in range(NC)
    ]


def groups(key):
    found = {}
    for z in range(NZ):
        for x in range(NX):
            for y in range(NY):
                for c in range(NC):
                    found.setdefault(key(z, x, y, c), []).append(device_index(z, x, y, c))
    return list(found.values())


def swap_cores(value):
    return lax.ppermute(value, AXES, permutation(lambda z, x, y, c: (z, x, y, 1 - c)))


def two_heads(rows):
    lane = lax.broadcasted_iota(jnp.int32, rows.shape, 1)
    wide = rows.astype(jnp.float32)
    first = jnp.where(lane < HEAD_DIM, wide, 0.0)
    second = jnp.where(lane < HEAD_DIM, 0.0, wide)
    return jnp.concatenate([first, second], axis=0).astype(jnp.bfloat16)


def live_grads(length_ref, grad):
    rows = grad.astype(jnp.float32)
    position = lax.broadcasted_iota(jnp.int32, rows.shape, 0)
    return two_heads(jnp.where(position < length_ref[0], rows, 0.0))


def dot_last(left, right):
    return lax.dot_general(left, right, (((1,), (1,)), ((), ())), preferred_element_type=jnp.float32)


def merged(rows, pairs):
    peak = jnp.max(rows[:, :pairs], axis=0)
    weight = jnp.exp2((rows[:, :pairs] - peak[None]) * EXP2_SCALE)
    total = jnp.sum(rows[:, pairs : 2 * pairs] * weight, axis=0)
    delta = jnp.sum(rows[:, 2 * pairs :] * weight, axis=0)
    return peak, total, delta


def stats_kernel(length_ref, query_ref, key_ref, value_ref, grad_ref, out_ref):
    for part in range(2):
        lanes = slice(part * PAIR, part * PAIR + PAIR)
        pair = 2 * pl.program_id(0) + part
        scores = dot_last(key_ref[:, lanes], two_heads(query_ref[:, lanes]))
        prob_grad = dot_last(value_ref[:, lanes], live_grads(length_ref, grad_ref[:, lanes]))
        peak = jnp.max(scores, axis=0, keepdims=True)
        expo = jnp.exp2((scores - peak) * EXP2_SCALE)
        out_ref[pl.ds(pair, 1), :] = peak
        out_ref[pl.ds(8 + pair, 1), :] = jnp.sum(expo, axis=0, keepdims=True)
        out_ref[pl.ds(16 + pair, 1), :] = jnp.sum(expo * prob_grad, axis=0, keepdims=True)


def merge_kernel(left_ref, right_ref, out_ref):
    pairs = out_ref.shape[0] // 3
    peak, total, delta = merged(jnp.stack([left_ref[...], right_ref[...]]), pairs)
    out_ref[:pairs] = peak
    out_ref[pairs : 2 * pairs] = total
    out_ref[2 * pairs :] = delta


def grads_kernel(first_pair, core_ref, length_ref, query_ref, key_ref, value_ref, grad_ref, *refs):
    stats_refs = refs[:2]
    joint_ref, mine_ref, sent_ref, query_kept_ref, query_sent_ref = refs[-5:]
    keeps_key = core_ref[0] == 0
    query_grads = []
    for part in range(2):
        lanes = slice(part * PAIR, part * PAIR + PAIR)
        pair = first_pair + 2 * pl.program_id(0) + part
        rows = jnp.stack([
            jnp.concatenate([ref[pl.ds(start + pair, 1), :] for start in (0, 8, 16)], axis=0)
            for ref in stats_refs
        ])
        peak, total, delta = merged(rows, 1)
        row_delta = delta / total
        inverse = 1.0 / total
        key = key_ref[:, lanes]
        queries = two_heads(query_ref[:, lanes])
        grads = live_grads(length_ref, grad_ref[:, lanes])
        scores = dot_last(key, queries)
        prob_grad = dot_last(value_ref[:, lanes], grads)
        prob = jnp.exp2((scores - peak) * EXP2_SCALE) * inverse
        prob_low = prob.astype(jnp.bfloat16)
        score_grad = (prob * (prob_grad - row_delta)).astype(jnp.bfloat16)
        value_grad = jnp.dot(prob_low, grads, preferred_element_type=jnp.float32)
        key_grad = jnp.dot(score_grad, queries, preferred_element_type=jnp.float32) * SCALE
        joint_ref[0, :, lanes] = key_grad.astype(jnp.bfloat16)
        joint_ref[1, :, lanes] = value_grad.astype(jnp.bfloat16)
        mine_ref[:, lanes] = jnp.where(keeps_key, key_grad, value_grad).astype(jnp.bfloat16)
        sent_ref[:, lanes] = jnp.where(keeps_key, value_grad, key_grad).astype(jnp.bfloat16)
        flipped = key.T
        answer = queries.shape[0] // 2
        query_grads.append(
            SCALE
            * jnp.concatenate(
                [
                    jnp.dot(flipped[:HEAD_DIM], score_grad[:, :answer], preferred_element_type=jnp.float32),
                    jnp.dot(flipped[HEAD_DIM:], score_grad[:, answer:], preferred_element_type=jnp.float32),
                ],
                axis=0,
            )
        )
    even, odd = query_grads
    query_kept_ref[0] = jnp.where(keeps_key, even, odd)
    query_sent_ref[0] = jnp.where(keeps_key, odd, even).astype(jnp.bfloat16)


def arrange_kernel(place_ref, *refs):
    shards, out_ref = refs[:-1], refs[-1]
    rows = shards[0].shape[1]
    for flip, shard in zip((0, 1, 3, 2), shards):
        first = pl.multiple_of(place_ref[flip] * rows, rows)
        out_ref[:, pl.ds(first, rows), :] = shard[...]


def split(place_ref, first, rows_of, refs):
    sides = len(refs) // 2
    for side, (near, far) in zip(range(sides), ((1, 3), (3, 1))):
        kept, sent = refs[2 * side : 2 * side + 2]
        for out, order in ((kept, (0, far)), (sent, (near, 2))):
            for index, flip in enumerate(order):
                rows_of(out.at[index], place_ref[first + flip], side)


def side_of(ref, index, rows, side, sides=2):
    part = ref.shape[-1] // sides
    return ref[index, rows, side * part : side * part + part]


def weights_kernel(place_ref, own_ref, other_ref, *refs):
    own_grads, other_grads, query_refs = refs[:2], refs[2:4], refs[4:8]
    x_outs, y_outs = refs[8:12], refs[12:16]
    x_total, y_total, query_total = refs[16:]
    own, other = own_ref[...].T, other_ref[...].T
    for total, own_grad, other_grad in zip((x_total, y_total), own_grads, other_grads):
        total[0] = jnp.dot(own, own_grad[...], preferred_element_type=jnp.float32) + jnp.dot(
            other, other_grad[...], preferred_element_type=jnp.float32
        )
    for y in range(NY):
        kept, received = query_refs[y // 2], query_refs[2 + y // 2]
        for side in range(2):
            first = pl.multiple_of(side * 64 + pl.program_id(0) * 16, 16)
            rows = kept[y % 2, pl.ds(first, 16), :] + received[y % 2, pl.ds(first, 16), :].astype(jnp.float32)
            query_total[y, side] = rows

    def x_rows(out, chosen, side):
        for z in range(out.shape[0]):
            rows = pl.ds(pl.multiple_of(z * 256 + chosen * 64, 64), 64)
            out[z] = side_of(x_total, 0, rows, side).astype(out.dtype)

    def y_rows(out, chosen, side):
        for z in range(NZ // 4):
            for x in range(NX):
                rows = pl.ds(pl.multiple_of(z * 256 + x * 64 + chosen * 16, 16), 16)
                row = (z * NX + x) * 16
                out[0, row : row + 16] = side_of(y_total, 0, rows, side).astype(out.dtype)
        out[0, NZ // 4 * NX * 16 :] = query_total[chosen, side].astype(out.dtype)

    split(place_ref, 0, x_rows, x_outs)
    split(place_ref, 4, y_rows, y_outs)


def middle_kernel(*refs):
    parts = len(refs) // 3
    for kept, received, out in zip(refs[:parts], refs[parts : 2 * parts], refs[2 * parts :]):
        out[...] = (kept[0] + received[0].astype(jnp.float32)).astype(out.dtype)


def add_parts(refs, total):
    sides = len(refs) // 3
    part = total.shape[-1] // sides
    for side in range(sides):
        kept, first, last = refs[side::sides]
        rows = kept[0] + first[0].astype(jnp.float32) + last[...].astype(jnp.float32)
        total[:, :, side * part : side * part + part] = rows


def second_kernel(place_ref, *refs):
    add_parts(refs[:6], refs[-2])
    add_parts(refs[6:12], refs[-1])
    x_outs, y_outs = refs[12:14], refs[14:16]
    query_out, x_total, y_total = refs[16:]
    query_out[...] = y_total[:, NZ // 4 * NX * 16 :]

    def x_rows(out, chosen, side):
        for z in range(NZ // 4):
            rows = pl.ds(pl.multiple_of(chosen * 16, 16), 16)
            out[z] = side_of(x_total, z, rows, side, 1).astype(out.dtype)

    def y_rows(out, chosen, side):
        for z in range(NZ // 4):
            rows = pl.ds(pl.multiple_of(z * NX * 16 + chosen * 16, 16), 16)
            out[z] = side_of(y_total, 0, rows, side, 1).astype(out.dtype)

    split(place_ref, 4, x_rows, x_outs)
    split(place_ref, 0, y_rows, y_outs)


def last_kernel(*refs):
    out, x_total, y_total = refs[6:]
    half = x_total.shape[2]
    add_parts(refs[:3], x_total)
    add_parts(refs[3:6], y_total)
    out[:, :, :half] = x_total[...].astype(out.dtype)
    out[:, :, half:] = y_total[...].astype(out.dtype)


def encoded_kernel(order_ref, *refs):
    grads, pieces, out_ref, results, sems = refs[0], refs[1:-3], *refs[-3:]
    stores = []
    for k, piece in enumerate(pieces):
        total = dot_last(grads[0], piece[0]) + dot_last(grads[1], piece[1])
        results[k] = total.astype(jnp.bfloat16)
        columns = pl.ds(pl.multiple_of(order_ref[k] * 256, 256), 256)
        store = pltpu.make_async_copy(results.at[k], out_ref.at[:, columns], sems.at[k])
        store.start()
        stores.append(store)
    for store in stores:
        store.wait()


def kernel_call(kernel, name, out_shape, mebibytes=12, flops=0, moved=0, **options):
    return pl.pallas_call(
        kernel,
        out_shape=out_shape,
        compiler_params=pltpu.CompilerParams(vmem_limit_bytes=mebibytes * MIB),
        cost_estimate=pl.CostEstimate(flops=flops, bytes_accessed=moved, transcendentals=0),
        name=name,
        **options,
    )


def like(shape, dtype):
    return jax.ShapeDtypeStruct(shape, dtype)


def along(axis, step):
    def target(z, x, y, c):
        return (
            z + step * (axis == "z"),
            x + step * (axis == "x"),
            y + step * (axis == "y"),
            c + step * (axis == "core"),
        )

    return permutation(target)


def send(value, links):
    return lax.ppermute(value, AXES, links)


def tie(value, *after):
    return lax.optimization_barrier((value, *after))[0]


def flipped(axis, bits):
    return permutation(lambda z, x, y, c: (z, x ^ bits if axis == "x" else x, y ^ bits if axis == "y" else y, c))


def halving(outs, axes, steps, beside=()):
    kept, sent = outs[0::2], outs[1::2]
    sides = len(kept) // 2
    ways = [(axis, *bits) for axis in axes for bits in ((1, 3), (3, 1))[:sides]]
    first = [send(value, flipped(axis, near)) for value, (axis, near, _) in zip(sent, ways)]
    first = lax.optimization_barrier(first)

    def block(shape):
        return pl.BlockSpec((1, shape[1] // steps, *shape[2:]), lambda i: (1, i, 0, 0))

    shapes = [value.shape for value in kept]
    middle = kernel_call(
        middle_kernel,
        "middle",
        [like(shape[1:], jnp.bfloat16) for shape in shapes],
        grid=(steps,),
        in_specs=[block(shape) for shape in shapes] * 2,
        out_specs=[pl.BlockSpec((shape[1] // steps, *shape[2:]), lambda i: (i, 0, 0)) for shape in shapes],
    )(*kept, *first)
    last = [send(value, flipped(axis, far)) for value, (axis, _, far) in zip(middle, ways)]
    last, beside = lax.optimization_barrier((last, beside))
    operands, specs = [], []
    for start in (0, sides):
        for values in (kept, first, last):
            for value in values[start : start + sides]:
                operands.append(value)
                inner = value.shape[-3:]
                shape = (1,) * (value.ndim - 3) + (inner[0] // steps, *inner[1:])
                leading = (0,) * (value.ndim - 3)
                specs.append(pl.BlockSpec(shape, lambda i, leading=leading: (*leading, i, 0, 0)))
    return operands, specs, middle[0], beside


def on_device(queries, key_rows, value_rows, encoded, key_weight, value_weight, grad_out, lengths):
    _, answer, features = queries.shape
    keys = key_rows.shape[1]
    width = encoded.shape[2]
    pairs = features // PAIR
    half = features // 2
    dp, passage = lax.axis_index("dp").astype(jnp.int32), lax.axis_index("passage").astype(jnp.int32)
    x_place, y_place, core = dp % NX, passage // NC, passage % NC
    place = jnp.stack([p ^ bits for p in (x_place, y_place) for bits in range(4)])
    queries, grad_out = queries[0], grad_out[0]
    key_rows, value_rows, encoded = key_rows[0], value_rows[0], encoded[0]
    f32, bf16 = jnp.float32, jnp.bfloat16
    smem = pl.BlockSpec(memory_space=pltpu.SMEM)

    shard = jnp.stack([key_weight, value_weight])
    shards = [shard] + [send(shard, flipped("x", bits)) for bits in (1, 3)]

    stats_shape = like((3 * pairs, 2 * answer), f32)
    row_spec = pl.BlockSpec((answer, 2 * PAIR), lambda p: (0, p))
    key_spec = pl.BlockSpec((keys, 2 * PAIR), lambda p: (0, p))
    stats = kernel_call(
        stats_kernel,
        "stats",
        pltpu.VMEM(stats_shape.shape, f32),
        62,
        grid=(pairs // 2,),
        in_specs=[smem, row_spec, key_spec, key_spec, row_spec],
        out_specs=pl.BlockSpec(stats_shape.shape, lambda p: (0, 0)),
    )(lengths, queries, key_rows, value_rows, grad_out)

    shards.append(send(tie(shards[1], stats), flipped("x", 3)))
    stats = kernel_call(merge_kernel, "merge", stats_shape)(stats, send(stats, along("core", 1)))
    met, encoded_other = lax.optimization_barrier((send(stats, flipped("y", 1)), swap_cores(encoded)))
    stats = kernel_call(merge_kernel, "merge", stats_shape)(stats, met)
    all_stats = [stats, send(stats, flipped("y", 3))]

    whole_vmem = pl.BlockSpec(memory_space=pltpu.VMEM)
    shards = lax.optimization_barrier((*shards, stats))[:-1]
    ordered = kernel_call(
        arrange_kernel,
        "arrange",
        like((2, NX * shard.shape[1], features), bf16),
        in_specs=[smem] + [whole_vmem] * NX,
        out_specs=whole_vmem,
    )(place, *shards)

    around = permutation(lambda z, x, y, c: (z + 1 - 2 * c, x, y, c))
    pieces = [ordered, send(ordered, around)]

    def grads(first_pair, joint):
        def rows(p):
            return (0, first_pair // 2 + p)

        row_spec = pl.BlockSpec((answer, 2 * PAIR), rows)
        key_spec = pl.BlockSpec((keys, 2 * PAIR), rows)
        out_spec = pl.BlockSpec((keys, 2 * PAIR), lambda p: (0, p))
        stats_spec = pl.BlockSpec(stats_shape.shape, lambda p: (0, 0))
        query_spec = pl.BlockSpec((1, PAIR, answer), lambda p: (p, 0, 0))
        joint_spec = pl.BlockSpec((2, keys, 2 * PAIR), lambda p: (0, 0, first_pair // 2 + p))
        operands = (core[None], lengths, queries, key_rows, value_rows, grad_out, *all_stats)
        specs = [smem, smem, row_spec, key_spec, key_spec, row_spec] + [stats_spec] * len(all_stats)
        aliases = {}
        if joint is not None:
            aliases = {len(operands): 0}
            operands += (joint,)
            specs.append(pl.BlockSpec(memory_space=pl.ANY))
        return kernel_call(
            functools.partial(grads_kernel, first_pair),
            "grads",
            [
                pltpu.HBM((2, keys, features), bf16),
                like((keys, half), bf16),
                like((keys, half), bf16),
                like((NY // 2, PAIR, answer), f32),
                like((NY // 2, PAIR, answer), bf16),
            ],
            grid=(pairs // 4,),
            in_specs=specs,
            out_specs=[joint_spec, out_spec, out_spec, query_spec, query_spec],
            input_output_aliases=aliases,
        )(*operands)

    joint, mine_a, sent_a, query_kept_a, query_sent_a = grads(0, None)
    received_a = swap_cores(sent_a)

    joint, mine_b, sent_b, query_kept_b, query_sent_b = grads(pairs // 2, joint)
    received_b = swap_cores(sent_b)
    query_received = [swap_cores(query_sent_a), swap_cores(query_sent_b)]

    def blocks(shape):
        return pl.BlockSpec((shape[0] // 4, *shape[1:]), lambda i: (i, 0, 0))

    whole = pl.BlockSpec((keys, half), lambda i: (0, 0))
    encoded_spec = pl.BlockSpec((keys, width // 4), lambda i: (0, i))
    query_spec = pl.BlockSpec(query_kept_a.shape, lambda i: (0, 0, 0))
    query_rows = PAIR * answer // half // 4
    x_shape = (2, NZ, 64, half // 2)
    y_shape = (2, 4, NZ // 4 * NX * 16 + query_rows, half // 2)

    def split_outs(shape, sides):
        spec = pl.BlockSpec((2, shape[1] // 4, *shape[2:]), lambda i: (0, i, 0, 0))
        return [like(shape, f32), like(shape, bf16)] * sides, [spec] * 2 * sides

    def total(shape):
        return pltpu.VMEM((shape[1] // 4, shape[2], 2 * shape[3]), f32)

    x_outs, x_specs = split_outs(x_shape, 2)
    y_outs, y_specs = split_outs(y_shape, 2)
    terms = kernel_call(
        weights_kernel,
        "weights",
        x_outs + y_outs,
        20,
        grid=(4,),
        in_specs=[smem, encoded_spec, encoded_spec] + [whole] * 4 + [query_spec] * 4,
        out_specs=x_specs + y_specs,
        scratch_shapes=[pltpu.VMEM((1, width // 4, half), f32)] * 2
        + [pltpu.VMEM((NY, 2, query_rows, answer), f32)],
    )(
        place,
        encoded,
        encoded_other,
        mine_a,
        mine_b,
        received_a,
        received_b,
        query_kept_a,
        query_kept_b,
        *query_received,
    )

    pieces.append(send(tie(pieces[1], terms[0]), around))

    operands, specs, middle, _ = halving(terms, "xy", 4)
    pieces.append(send(tie(pieces[2], middle), around))
    chunk, query_shape = (2, NZ, 16, half), (4, query_rows, half)
    chunk_outs, chunk_specs = split_outs(chunk, 1)
    *second, query_grad = kernel_call(
        second_kernel,
        "second",
        chunk_outs * 2 + [like(query_shape, f32)],
        grid=(4,),
        in_specs=[smem] + specs,
        out_specs=chunk_specs * 2 + [blocks(query_shape)],
        scratch_shapes=[total(x_shape), total(y_shape)],
    )(place, *operands)
    query_grad = query_grad.reshape(4, query_rows, 2, answer).transpose(2, 0, 1, 3)
    query_grad = query_grad.reshape(PAIR, answer).T.astype(bf16)[None]

    across = send(tie(pieces[3], second[0]), around)
    operands, specs, _, across = halving(second, "yx", 1, across)
    last = kernel_call(
        last_kernel,
        "last",
        like((NZ, 16, features), bf16),
        grid=(1,),
        in_specs=specs,
        out_specs=pl.BlockSpec((NZ, 16, features), lambda i: (0, 0, 0)),
        scratch_shapes=[pltpu.VMEM((NZ, 16, half), f32)] * 2,
    )(*operands)
    swapped = [swap_cores(tie(piece, last)) for piece in pieces[1:4]]
    last = lax.all_to_all(
        last.reshape(NZ * NC, 8, features),
        AXES,
        0,
        0,
        tiled=True,
        axis_index_groups=groups(lambda z, x, y, c: (x, y)),
    )

    z_place, way = dp // NX, 1 - 2 * core
    order = [(z_place + way * step + NZ) % NZ for step in (0, -1, -2, -3, 1, 2, 3, 4)]
    in_hbm = pl.BlockSpec(memory_space=pltpu.HBM)
    encoded_grad = kernel_call(
        encoded_kernel,
        "encoded",
        pltpu.HBM((keys, width), bf16),
        24,
        flops=4 * keys * width * features,
        moved=14 * MIB,
        in_specs=[smem] + [whole_vmem] * (NZ + 1),
        out_specs=in_hbm,
        scratch_shapes=[
            pltpu.VMEM((NZ, keys, width // NZ), bf16),
            pltpu.SemaphoreType.DMA((NZ,)),
        ],
    )(jnp.stack(order), joint, *pieces, *swapped, across)
    summed = tie(last, encoded_grad).reshape(NZ, NC, 8, features).astype(f32).sum(0)
    key_weight_grad, value_weight_grad = summed[0], summed[1]
    return query_grad, encoded_grad[None], key_weight_grad, value_weight_grad


def solution(mesh):
    return jax.shard_map(
        on_device,
        mesh=mesh,
        in_specs=(
            P("dp", None, None),
            P("dp", "passage", None),
            P("dp", "passage", None),
            P("dp", "passage", None),
            P("dp", None),
            P("dp", None),
            P("dp", None, None),
            P("dp"),
        ),
        out_specs=(
            P("dp", None, "passage"),
            P("dp", "passage", None),
            P(("dp", "passage"), None),
            P(("dp", "passage"), None),
        ),
        check_vma=False,
    )
```

```python
import functools
import math

import jax
import jax.numpy as jnp
from jax import lax
from jax.experimental import pallas as pl
from jax.experimental.pallas import tpu as pltpu
from jax.sharding import PartitionSpec as P

HEADS = 16
HEAD_DIM = 64
PAIR = 2 * HEAD_DIM
SCALE = 1.0 / math.sqrt(HEAD_DIM)
EXP2_SCALE = SCALE * math.log2(math.e)
NZ, NX, NY, NC = 8, 4, 4, 2
AXES = ("dp", "passage")
MIB = 1024 * 1024


def device_index(z, x, y, c):
    return ((z % NZ) * NX + x % NX) * (NY * NC) + (y % NY) * NC + c % NC


def permutation(target):
    return [
        (device_index(z, x, y, c), device_index(*target(z, x, y, c)))
        for z in range(NZ)
        for x in range(NX)
        for y in range(NY)
        for c in range(NC)
    ]


def groups(key):
    found = {}
    for z in range(NZ):
        for x in range(NX):
            for y in range(NY):
                for c in range(NC):
                    found.setdefault(key(z, x, y, c), []).append(device_index(z, x, y, c))
    return list(found.values())


def swap_cores(value):
    return lax.ppermute(value, AXES, permutation(lambda z, x, y, c: (z, x, y, 1 - c)))


def two_heads(rows):
    lane = lax.broadcasted_iota(jnp.int32, rows.shape, 1)
    wide = rows.astype(jnp.float32)
    first = jnp.where(lane < HEAD_DIM, wide, 0.0)
    second = jnp.where(lane < HEAD_DIM, 0.0, wide)
    return jnp.concatenate([first, second], axis=0).astype(jnp.bfloat16)


def live_grads(length_ref, grad):
    rows = grad.astype(jnp.float32)
    position = lax.broadcasted_iota(jnp.int32, rows.shape, 0)
    return two_heads(jnp.where(position < length_ref[0], rows, 0.0))


def dot_last(left, right):
    return lax.dot_general(left, right, (((1,), (1,)), ((), ())), preferred_element_type=jnp.float32)


def merged(rows, pairs):
    peak = jnp.max(rows[:, :pairs], axis=0)
    weight = jnp.exp2((rows[:, :pairs] - peak[None]) * EXP2_SCALE)
    total = jnp.sum(rows[:, pairs : 2 * pairs] * weight, axis=0)
    delta = jnp.sum(rows[:, 2 * pairs :] * weight, axis=0)
    return peak, total, delta


def stats_kernel(length_ref, query_ref, key_ref, value_ref, grad_ref, out_ref):
    for part in range(2):
        lanes = slice(part * PAIR, part * PAIR + PAIR)
        pair = 2 * pl.program_id(0) + part
        scores = dot_last(key_ref[:, lanes], two_heads(query_ref[:, lanes]))
        prob_grad = dot_last(value_ref[:, lanes], live_grads(length_ref, grad_ref[:, lanes]))
        peak = jnp.max(scores, axis=0, keepdims=True)
        expo = jnp.exp2((scores - peak) * EXP2_SCALE)
        out_ref[pl.ds(pair, 1), :] = peak
        out_ref[pl.ds(8 + pair, 1), :] = jnp.sum(expo, axis=0, keepdims=True)
        out_ref[pl.ds(16 + pair, 1), :] = jnp.sum(expo * prob_grad, axis=0, keepdims=True)


def merge_kernel(left_ref, right_ref, out_ref):
    pairs = out_ref.shape[0] // 3
    peak, total, delta = merged(jnp.stack([left_ref[...], right_ref[...]]), pairs)
    out_ref[:pairs] = peak
    out_ref[pairs : 2 * pairs] = total
    out_ref[2 * pairs :] = delta


def grads_kernel(first_pair, core_ref, length_ref, query_ref, key_ref, value_ref, grad_ref, *refs):
    stats_refs = refs[:2]
    joint_ref, mine_ref, sent_ref, query_kept_ref, query_sent_ref = refs[-5:]
    keeps_key = core_ref[0] == 0
    query_grads = []
    for part in range(2):
        lanes = slice(part * PAIR, part * PAIR + PAIR)
        pair = first_pair + 2 * pl.program_id(0) + part
        rows = jnp.stack([
            jnp.concatenate([ref[pl.ds(start + pair, 1), :] for start in (0, 8, 16)], axis=0)
            for ref in stats_refs
        ])
        peak, total, delta = merged(rows, 1)
        row_delta = delta / total
        inverse = 1.0 / total
        key = key_ref[:, lanes]
        queries = two_heads(query_ref[:, lanes])
        grads = live_grads(length_ref, grad_ref[:, lanes])
        scores = dot_last(key, queries)
        prob_grad = dot_last(value_ref[:, lanes], grads)
        prob = jnp.exp2((scores - peak) * EXP2_SCALE) * inverse
        prob_low = prob.astype(jnp.bfloat16)
        score_grad = (prob * (prob_grad - row_delta)).astype(jnp.bfloat16)
        value_grad = jnp.dot(prob_low, grads, preferred_element_type=jnp.float32)
        key_grad = jnp.dot(score_grad, queries, preferred_element_type=jnp.float32) * SCALE
        joint_ref[0, :, lanes] = key_grad.astype(jnp.bfloat16)
        joint_ref[1, :, lanes] = value_grad.astype(jnp.bfloat16)
        mine_ref[:, lanes] = jnp.where(keeps_key, key_grad, value_grad).astype(jnp.bfloat16)
        sent_ref[:, lanes] = jnp.where(keeps_key, value_grad, key_grad).astype(jnp.bfloat16)
        flipped = key.T
        answer = queries.shape[0] // 2
        query_grads.append(
            SCALE
            * jnp.concatenate(
                [
                    jnp.dot(flipped[:HEAD_DIM], score_grad[:, :answer], preferred_element_type=jnp.float32),
                    jnp.dot(flipped[HEAD_DIM:], score_grad[:, answer:], preferred_element_type=jnp.float32),
                ],
                axis=0,
            )
        )
    even, odd = query_grads
    query_kept_ref[0] = jnp.where(keeps_key, even, odd)
    query_sent_ref[0] = jnp.where(keeps_key, odd, even).astype(jnp.bfloat16)


def arrange_kernel(place_ref, *refs):
    shards, out_ref = refs[:-1], refs[-1]
    rows = shards[0].shape[1]
    for flip, shard in zip((0, 1, 3, 2), shards):
        first = pl.multiple_of(place_ref[flip] * rows, rows)
        out_ref[:, pl.ds(first, rows), :] = shard[...]


def split(place_ref, first, rows_of, refs):
    sides = len(refs) // 2
    for side, (near, far) in zip(range(sides), ((1, 3), (3, 1))):
        kept, sent = refs[2 * side : 2 * side + 2]
        for out, order in ((kept, (0, far)), (sent, (near, 2))):
            for index, flip in enumerate(order):
                rows_of(out.at[index], place_ref[first + flip], side)


def side_of(ref, index, rows, side, sides=2):
    part = ref.shape[-1] // sides
    return ref[index, rows, side * part : side * part + part]


def weights_kernel(place_ref, own_ref, other_ref, *refs):
    own_grads, other_grads, query_refs = refs[:2], refs[2:4], refs[4:8]
    x_outs, y_outs = refs[8:12], refs[12:16]
    x_total, y_total, query_total = refs[16:]
    own, other = own_ref[...].T, other_ref[...].T
    for total, own_grad, other_grad in zip((x_total, y_total), own_grads, other_grads):
        total[0] = jnp.dot(own, own_grad[...], preferred_element_type=jnp.float32) + jnp.dot(
            other, other_grad[...], preferred_element_type=jnp.float32
        )
    for y in range(NY):
        kept, received = query_refs[y // 2], query_refs[2 + y // 2]
        for side in range(2):
            first = pl.multiple_of(side * 64 + pl.program_id(0) * 16, 16)
            rows = kept[y % 2, pl.ds(first, 16), :] + received[y % 2, pl.ds(first, 16), :].astype(jnp.float32)
            query_total[y, side] = rows

    def x_rows(out, chosen, side):
        for z in range(out.shape[0]):
            rows = pl.ds(pl.multiple_of(z * 256 + chosen * 64, 64), 64)
            out[z] = side_of(x_total, 0, rows, side).astype(out.dtype)

    def y_rows(out, chosen, side):
        for z in range(NZ // 4):
            for x in range(NX):
                rows = pl.ds(pl.multiple_of(z * 256 + x * 64 + chosen * 16, 16), 16)
                row = (z * NX + x) * 16
                out[0, row : row + 16] = side_of(y_total, 0, rows, side).astype(out.dtype)
        out[0, NZ // 4 * NX * 16 :] = query_total[chosen, side].astype(out.dtype)

    split(place_ref, 0, x_rows, x_outs)
    split(place_ref, 4, y_rows, y_outs)


def middle_kernel(*refs):
    parts = len(refs) // 3
    for kept, received, out in zip(refs[:parts], refs[parts : 2 * parts], refs[2 * parts :]):
        out[...] = (kept[0] + received[0].astype(jnp.float32)).astype(out.dtype)


def add_parts(refs, total):
    sides = len(refs) // 3
    part = total.shape[-1] // sides
    for side in range(sides):
        kept, first, last = refs[side::sides]
        rows = kept[0] + first[0].astype(jnp.float32) + last[...].astype(jnp.float32)
        total[:, :, side * part : side * part + part] = rows


def second_kernel(place_ref, *refs):
    add_parts(refs[:6], refs[-2])
    add_parts(refs[6:12], refs[-1])
    x_outs, y_outs = refs[12:14], refs[14:16]
    query_out, x_total, y_total = refs[16:]
    query_out[...] = y_total[:, NZ // 4 * NX * 16 :]

    def x_rows(out, chosen, side):
        for z in range(NZ // 4):
            rows = pl.ds(pl.multiple_of(chosen * 16, 16), 16)
            out[z] = side_of(x_total, z, rows, side, 1).astype(out.dtype)

    def y_rows(out, chosen, side):
        for z in range(NZ // 4):
            rows = pl.ds(pl.multiple_of(z * NX * 16 + chosen * 16, 16), 16)
            out[z] = side_of(y_total, 0, rows, side, 1).astype(out.dtype)

    split(place_ref, 4, x_rows, x_outs)
    split(place_ref, 0, y_rows, y_outs)


def last_kernel(*refs):
    out, x_total, y_total = refs[6:]
    half = x_total.shape[2]
    add_parts(refs[:3], x_total)
    add_parts(refs[3:6], y_total)
    out[:, :, :half] = x_total[...].astype(out.dtype)
    out[:, :, half:] = y_total[...].astype(out.dtype)


def encoded_kernel(order_ref, *refs):
    grads, pieces, out_ref, results, sems = refs[0], refs[1:-3], *refs[-3:]
    stores = []
    for k, piece in enumerate(pieces):
        total = dot_last(grads[0], piece[0]) + dot_last(grads[1], piece[1])
        results[k] = total.astype(jnp.bfloat16)
        columns = pl.ds(pl.multiple_of(order_ref[k] * 256, 256), 256)
        store = pltpu.make_async_copy(results.at[k], out_ref.at[:, columns], sems.at[k])
        store.start()
        stores.append(store)
    for store in stores:
        store.wait()


def kernel_call(kernel, name, out_shape, mebibytes=12, flops=0, moved=0, **options):
    return pl.pallas_call(
        kernel,
        out_shape=out_shape,
        compiler_params=pltpu.CompilerParams(vmem_limit_bytes=mebibytes * MIB),
        cost_estimate=pl.CostEstimate(flops=flops, bytes_accessed=moved, transcendentals=0),
        name=name,
        **options,
    )


def like(shape, dtype):
    return jax.ShapeDtypeStruct(shape, dtype)


def along(axis, step):
    def target(z, x, y, c):
        return (
            z + step * (axis == "z"),
            x + step * (axis == "x"),
            y + step * (axis == "y"),
            c + step * (axis == "core"),
        )

    return permutation(target)


def send(value, links):
    return lax.ppermute(value, AXES, links)


def tie(value, *after):
    return lax.optimization_barrier((value, *after))[0]


def flipped(axis, bits):
    return permutation(lambda z, x, y, c: (z, x ^ bits if axis == "x" else x, y ^ bits if axis == "y" else y, c))


def halving(outs, axes, steps, beside=()):
    kept, sent = outs[0::2], outs[1::2]
    sides = len(kept) // 2
    ways = [(axis, *bits) for axis in axes for bits in ((1, 3), (3, 1))[:sides]]
    first = [send(value, flipped(axis, near)) for value, (axis, near, _) in zip(sent, ways)]
    first = lax.optimization_barrier(first)

    def block(shape):
        return pl.BlockSpec((1, shape[1] // steps, *shape[2:]), lambda i: (1, i, 0, 0))

    shapes = [value.shape for value in kept]
    middle = kernel_call(
        middle_kernel,
        "middle",
        [like(shape[1:], jnp.bfloat16) for shape in shapes],
        grid=(steps,),
        in_specs=[block(shape) for shape in shapes] * 2,
        out_specs=[pl.BlockSpec((shape[1] // steps, *shape[2:]), lambda i: (i, 0, 0)) for shape in shapes],
    )(*kept, *first)
    last = [send(value, flipped(axis, far)) for value, (axis, _, far) in zip(middle, ways)]
    last, beside = lax.optimization_barrier((last, beside))
    operands, specs = [], []
    for start in (0, sides):
        for values in (kept, first, last):
            for value in values[start : start + sides]:
                operands.append(value)
                inner = value.shape[-3:]
                shape = (1,) * (value.ndim - 3) + (inner[0] // steps, *inner[1:])
                leading = (0,) * (value.ndim - 3)
                specs.append(pl.BlockSpec(shape, lambda i, leading=leading: (*leading, i, 0, 0)))
    return operands, specs, middle[0], beside


def on_device(queries, key_rows, value_rows, encoded, key_weight, value_weight, grad_out, lengths):
    _, answer, features = queries.shape
    keys = key_rows.shape[1]
    width = encoded.shape[2]
    pairs = features // PAIR
    half = features // 2
    dp, passage = lax.axis_index("dp").astype(jnp.int32), lax.axis_index("passage").astype(jnp.int32)
    x_place, y_place, core = dp % NX, passage // NC, passage % NC
    place = jnp.stack([p ^ bits for p in (x_place, y_place) for bits in range(4)])
    queries, grad_out = queries[0], grad_out[0]
    key_rows, value_rows, encoded = key_rows[0], value_rows[0], encoded[0]
    f32, bf16 = jnp.float32, jnp.bfloat16
    smem = pl.BlockSpec(memory_space=pltpu.SMEM)

    shard = jnp.stack([key_weight, value_weight])
    shards = [shard] + [send(shard, flipped("x", bits)) for bits in (1, 3)]

    stats_shape = like((3 * pairs, 2 * answer), f32)
    row_spec = pl.BlockSpec((answer, 2 * PAIR), lambda p: (0, p))
    key_spec = pl.BlockSpec((keys, 2 * PAIR), lambda p: (0, p))
    stats = kernel_call(
        stats_kernel,
        "stats",
        pltpu.VMEM(stats_shape.shape, f32),
        62,
        grid=(pairs // 2,),
        in_specs=[smem, row_spec, key_spec, key_spec, row_spec],
        out_specs=pl.BlockSpec(stats_shape.shape, lambda p: (0, 0)),
    )(lengths, queries, key_rows, value_rows, grad_out)

    shards.append(send(tie(shards[1], stats), flipped("x", 3)))
    stats = kernel_call(merge_kernel, "merge", stats_shape)(stats, send(stats, along("core", 1)))
    met, encoded_other = lax.optimization_barrier((send(stats, flipped("y", 1)), swap_cores(encoded)))
    stats = kernel_call(merge_kernel, "merge", stats_shape)(stats, met)
    all_stats = [stats, send(stats, flipped("y", 3))]

    whole_vmem = pl.BlockSpec(memory_space=pltpu.VMEM)
    shards = lax.optimization_barrier((*shards, all_stats[1]))[:-1]
    ordered = kernel_call(
        arrange_kernel,
        "arrange",
        like((2, NX * shard.shape[1], features), bf16),
        in_specs=[smem] + [whole_vmem] * NX,
        out_specs=whole_vmem,
    )(place, *shards)

    around = permutation(lambda z, x, y, c: (z + 1 - 2 * c, x, y, c))
    pieces = [ordered, send(ordered, around)]

    def grads(first_pair, joint):
        def rows(p):
            return (0, first_pair // 2 + p)

        row_spec = pl.BlockSpec((answer, 2 * PAIR), rows)
        key_spec = pl.BlockSpec((keys, 2 * PAIR), rows)
        out_spec = pl.BlockSpec((keys, 2 * PAIR), lambda p: (0, p))
        stats_spec = pl.BlockSpec(stats_shape.shape, lambda p: (0, 0))
        query_spec = pl.BlockSpec((1, PAIR, answer), lambda p: (p, 0, 0))
        joint_spec = pl.BlockSpec((2, keys, 2 * PAIR), lambda p: (0, 0, first_pair // 2 + p))
        operands = (core[None], lengths, queries, key_rows, value_rows, grad_out, *all_stats)
        specs = [smem, smem, row_spec, key_spec, key_spec, row_spec] + [stats_spec] * len(all_stats)
        aliases = {}
        if joint is not None:
            aliases = {len(operands): 0}
            operands += (joint,)
            specs.append(pl.BlockSpec(memory_space=pl.ANY))
        return kernel_call(
            functools.partial(grads_kernel, first_pair),
            "grads",
            [
                pltpu.HBM((2, keys, features), bf16),
                like((keys, half), bf16),
                like((keys, half), bf16),
                like((NY // 2, PAIR, answer), f32),
                like((NY // 2, PAIR, answer), bf16),
            ],
            grid=(pairs // 4,),
            in_specs=specs,
            out_specs=[joint_spec, out_spec, out_spec, query_spec, query_spec],
            input_output_aliases=aliases,
        )(*operands)

    joint, mine_a, sent_a, query_kept_a, query_sent_a = grads(0, None)
    received_a = swap_cores(sent_a)

    joint, mine_b, sent_b, query_kept_b, query_sent_b = grads(pairs // 2, joint)
    received_b = swap_cores(sent_b)
    query_received = [swap_cores(query_sent_a), swap_cores(query_sent_b)]

    def blocks(shape):
        return pl.BlockSpec((shape[0] // 4, *shape[1:]), lambda i: (i, 0, 0))

    whole = pl.BlockSpec((keys, half), lambda i: (0, 0))
    encoded_spec = pl.BlockSpec((keys, width // 4), lambda i: (0, i))
    query_spec = pl.BlockSpec(query_kept_a.shape, lambda i: (0, 0, 0))
    query_rows = PAIR * answer // half // 4
    x_shape = (2, NZ, 64, half // 2)
    y_shape = (2, 4, NZ // 4 * NX * 16 + query_rows, half // 2)

    def split_outs(shape, sides):
        spec = pl.BlockSpec((2, shape[1] // 4, *shape[2:]), lambda i: (0, i, 0, 0))
        return [like(shape, f32), like(shape, bf16)] * sides, [spec] * 2 * sides

    def total(shape):
        return pltpu.VMEM((shape[1] // 4, shape[2], 2 * shape[3]), f32)

    x_outs, x_specs = split_outs(x_shape, 2)
    y_outs, y_specs = split_outs(y_shape, 2)
    terms = kernel_call(
        weights_kernel,
        "weights",
        x_outs + y_outs,
        20,
        grid=(4,),
        in_specs=[smem, encoded_spec, encoded_spec] + [whole] * 4 + [query_spec] * 4,
        out_specs=x_specs + y_specs,
        scratch_shapes=[pltpu.VMEM((1, width // 4, half), f32)] * 2
        + [pltpu.VMEM((NY, 2, query_rows, answer), f32)],
    )(
        place,
        encoded,
        encoded_other,
        mine_a,
        mine_b,
        received_a,
        received_b,
        query_kept_a,
        query_kept_b,
        *query_received,
    )

    pieces.append(send(tie(pieces[1], terms[0]), around))

    operands, specs, middle, _ = halving(terms, "xy", 4)
    pieces.append(send(tie(pieces[2], middle), around))
    chunk, query_shape = (2, NZ, 16, half), (4, query_rows, half)
    chunk_outs, chunk_specs = split_outs(chunk, 1)
    *second, query_grad = kernel_call(
        second_kernel,
        "second",
        chunk_outs * 2 + [like(query_shape, f32)],
        grid=(4,),
        in_specs=[smem] + specs,
        out_specs=chunk_specs * 2 + [blocks(query_shape)],
        scratch_shapes=[total(x_shape), total(y_shape)],
    )(place, *operands)
    query_grad = query_grad.reshape(4, query_rows, 2, answer).transpose(2, 0, 1, 3)
    query_grad = query_grad.reshape(PAIR, answer).T.astype(bf16)[None]

    across = send(tie(pieces[3], second[0]), around)
    operands, specs, _, across = halving(second, "yx", 1, across)
    last = kernel_call(
        last_kernel,
        "last",
        like((NZ, 16, features), bf16),
        grid=(1,),
        in_specs=specs,
        out_specs=pl.BlockSpec((NZ, 16, features), lambda i: (0, 0, 0)),
        scratch_shapes=[pltpu.VMEM((NZ, 16, half), f32)] * 2,
    )(*operands)
    swapped = [swap_cores(tie(piece, last)) for piece in pieces[1:4]]
    last = lax.all_to_all(
        last.reshape(NZ * NC, 8, features),
        AXES,
        0,
        0,
        tiled=True,
        axis_index_groups=groups(lambda z, x, y, c: (x, y)),
    )

    z_place, way = dp // NX, 1 - 2 * core
    order = [(z_place + way * step + NZ) % NZ for step in (0, -1, -2, -3, 1, 2, 3, 4)]
    in_hbm = pl.BlockSpec(memory_space=pltpu.HBM)
    encoded_grad = kernel_call(
        encoded_kernel,
        "encoded",
        pltpu.HBM((keys, width), bf16),
        24,
        flops=4 * keys * width * features,
        moved=14 * MIB,
        in_specs=[smem] + [whole_vmem] * (NZ + 1),
        out_specs=in_hbm,
        scratch_shapes=[
            pltpu.VMEM((NZ, keys, width // NZ), bf16),
            pltpu.SemaphoreType.DMA((NZ,)),
        ],
    )(jnp.stack(order), joint, *pieces, *swapped, across)
    summed = tie(last, encoded_grad).reshape(NZ, NC, 8, features).astype(f32).sum(0)
    key_weight_grad, value_weight_grad = summed[0], summed[1]
    return query_grad, encoded_grad[None], key_weight_grad, value_weight_grad


def solution(mesh):
    return jax.shard_map(
        on_device,
        mesh=mesh,
        in_specs=(
            P("dp", None, None),
            P("dp", "passage", None),
            P("dp", "passage", None),
            P("dp", "passage", None),
            P("dp", None),
            P("dp", None),
            P("dp", None, None),
            P("dp"),
        ),
        out_specs=(
            P("dp", None, "passage"),
            P("dp", "passage", None),
            P(("dp", "passage"), None),
            P(("dp", "passage"), None),
        ),
        check_vma=False,
    )
```

```python
import functools
import math

import jax
import jax.numpy as jnp
from jax import lax
from jax.experimental import pallas as pl
from jax.experimental.pallas import tpu as pltpu
from jax.sharding import PartitionSpec as P

HEADS = 16
HEAD_DIM = 64
PAIR = 2 * HEAD_DIM
SCALE = 1.0 / math.sqrt(HEAD_DIM)
EXP2_SCALE = SCALE * math.log2(math.e)
NZ, NX, NY, NC = 8, 4, 4, 2
AXES = ("dp", "passage")
MIB = 1024 * 1024


def device_index(z, x, y, c):
    return ((z % NZ) * NX + x % NX) * (NY * NC) + (y % NY) * NC + c % NC


def permutation(target):
    return [
        (device_index(z, x, y, c), device_index(*target(z, x, y, c)))
        for z in range(NZ)
        for x in range(NX)
        for y in range(NY)
        for c in range(NC)
    ]


def groups(key):
    found = {}
    for z in range(NZ):
        for x in range(NX):
            for y in range(NY):
                for c in range(NC):
                    found.setdefault(key(z, x, y, c), []).append(device_index(z, x, y, c))
    return list(found.values())


def swap_cores(value):
    return lax.ppermute(value, AXES, permutation(lambda z, x, y, c: (z, x, y, 1 - c)))


def two_heads(rows):
    lane = lax.broadcasted_iota(jnp.int32, rows.shape, 1)
    wide = rows.astype(jnp.float32)
    first = jnp.where(lane < HEAD_DIM, wide, 0.0)
    second = jnp.where(lane < HEAD_DIM, 0.0, wide)
    return jnp.concatenate([first, second], axis=0).astype(jnp.bfloat16)


def live_grads(length_ref, grad):
    rows = grad.astype(jnp.float32)
    position = lax.broadcasted_iota(jnp.int32, rows.shape, 0)
    return two_heads(jnp.where(position < length_ref[0], rows, 0.0))


def dot_last(left, right):
    return lax.dot_general(left, right, (((1,), (1,)), ((), ())), preferred_element_type=jnp.float32)


def merged(rows, pairs):
    peak = jnp.max(rows[:, :pairs], axis=0)
    weight = jnp.exp2((rows[:, :pairs] - peak[None]) * EXP2_SCALE)
    total = jnp.sum(rows[:, pairs : 2 * pairs] * weight, axis=0)
    delta = jnp.sum(rows[:, 2 * pairs :] * weight, axis=0)
    return peak, total, delta


def stats_kernel(length_ref, query_ref, key_ref, value_ref, grad_ref, out_ref):
    for part in range(2):
        lanes = slice(part * PAIR, part * PAIR + PAIR)
        pair = 2 * pl.program_id(0) + part
        scores = dot_last(key_ref[:, lanes], two_heads(query_ref[:, lanes]))
        prob_grad = dot_last(value_ref[:, lanes], live_grads(length_ref, grad_ref[:, lanes]))
        peak = jnp.max(scores, axis=0, keepdims=True)
        expo = jnp.exp2((scores - peak) * EXP2_SCALE)
        out_ref[pl.ds(pair, 1), :] = peak
        out_ref[pl.ds(8 + pair, 1), :] = jnp.sum(expo, axis=0, keepdims=True)
        out_ref[pl.ds(16 + pair, 1), :] = jnp.sum(expo * prob_grad, axis=0, keepdims=True)


def merge_kernel(left_ref, right_ref, out_ref):
    pairs = out_ref.shape[0] // 3
    peak, total, delta = merged(jnp.stack([left_ref[...], right_ref[...]]), pairs)
    out_ref[:pairs] = peak
    out_ref[pairs : 2 * pairs] = total
    out_ref[2 * pairs :] = delta


def grads_kernel(first_pair, core_ref, length_ref, query_ref, key_ref, value_ref, grad_ref, *refs):
    stats_refs = refs[:2]
    joint_ref, mine_ref, sent_ref, query_kept_ref, query_sent_ref = refs[-5:]
    keeps_key = core_ref[0] == 0
    query_grads = []
    for part in range(2):
        lanes = slice(part * PAIR, part * PAIR + PAIR)
        pair = first_pair + 2 * pl.program_id(0) + part
        rows = jnp.stack([
            jnp.concatenate([ref[pl.ds(start + pair, 1), :] for start in (0, 8, 16)], axis=0)
            for ref in stats_refs
        ])
        peak, total, delta = merged(rows, 1)
        row_delta = delta / total
        inverse = 1.0 / total
        key = key_ref[:, lanes]
        queries = two_heads(query_ref[:, lanes])
        grads = live_grads(length_ref, grad_ref[:, lanes])
        scores = dot_last(key, queries)
        prob_grad = dot_last(value_ref[:, lanes], grads)
        prob = jnp.exp2((scores - peak) * EXP2_SCALE) * inverse
        prob_low = prob.astype(jnp.bfloat16)
        score_grad = (prob * (prob_grad - row_delta)).astype(jnp.bfloat16)
        value_grad = jnp.dot(prob_low, grads, preferred_element_type=jnp.float32)
        key_grad = jnp.dot(score_grad, queries, preferred_element_type=jnp.float32) * SCALE
        joint_ref[0, :, lanes] = key_grad.astype(jnp.bfloat16)
        joint_ref[1, :, lanes] = value_grad.astype(jnp.bfloat16)
        mine_ref[:, lanes] = jnp.where(keeps_key, key_grad, value_grad).astype(jnp.bfloat16)
        sent_ref[:, lanes] = jnp.where(keeps_key, value_grad, key_grad).astype(jnp.bfloat16)
        flipped = key.T
        answer = queries.shape[0] // 2
        query_grads.append(
            SCALE
            * jnp.concatenate(
                [
                    jnp.dot(flipped[:HEAD_DIM], score_grad[:, :answer], preferred_element_type=jnp.float32),
                    jnp.dot(flipped[HEAD_DIM:], score_grad[:, answer:], preferred_element_type=jnp.float32),
                ],
                axis=0,
            )
        )
    even, odd = query_grads
    query_kept_ref[0] = jnp.where(keeps_key, even, odd)
    query_sent_ref[0] = jnp.where(keeps_key, odd, even).astype(jnp.bfloat16)


def arrange_kernel(place_ref, *refs):
    shards, out_ref = refs[:-1], refs[-1]
    rows = shards[0].shape[1]
    for flip, shard in zip((0, 1, 3, 2), shards):
        first = pl.multiple_of(place_ref[flip] * rows, rows)
        out_ref[:, pl.ds(first, rows), :] = shard[...]


def split(place_ref, first, rows_of, refs):
    sides = len(refs) // 2
    for side, (near, far) in zip(range(sides), ((1, 3), (3, 1))):
        kept, sent = refs[2 * side : 2 * side + 2]
        for out, order in ((kept, (0, far)), (sent, (near, 2))):
            for index, flip in enumerate(order):
                rows_of(out.at[index], place_ref[first + flip], side)


def side_of(ref, index, rows, side, sides=2):
    part = ref.shape[-1] // sides
    return ref[index, rows, side * part : side * part + part]


def weights_kernel(place_ref, own_ref, other_ref, *refs):
    own_grads, other_grads, query_refs = refs[:2], refs[2:4], refs[4:8]
    x_outs, y_outs = refs[8:12], refs[12:16]
    x_total, y_total, query_total = refs[16:]
    own, other = own_ref[...].T, other_ref[...].T
    for total, own_grad, other_grad in zip((x_total, y_total), own_grads, other_grads):
        total[0] = jnp.dot(own, own_grad[...], preferred_element_type=jnp.float32) + jnp.dot(
            other, other_grad[...], preferred_element_type=jnp.float32
        )
    for y in range(NY):
        kept, received = query_refs[y // 2], query_refs[2 + y // 2]
        for side in range(2):
            first = pl.multiple_of(side * 64 + pl.program_id(0) * 16, 16)
            rows = kept[y % 2, pl.ds(first, 16), :] + received[y % 2, pl.ds(first, 16), :].astype(jnp.float32)
            query_total[y, side] = rows

    def x_rows(out, chosen, side):
        for z in range(out.shape[0]):
            rows = pl.ds(pl.multiple_of(z * 256 + chosen * 64, 64), 64)
            out[z] = side_of(x_total, 0, rows, side).astype(out.dtype)

    def y_rows(out, chosen, side):
        for z in range(NZ // 4):
            for x in range(NX):
                rows = pl.ds(pl.multiple_of(z * 256 + x * 64 + chosen * 16, 16), 16)
                row = (z * NX + x) * 16
                out[0, row : row + 16] = side_of(y_total, 0, rows, side).astype(out.dtype)
        out[0, NZ // 4 * NX * 16 :] = query_total[chosen, side].astype(out.dtype)

    split(place_ref, 0, x_rows, x_outs)
    split(place_ref, 4, y_rows, y_outs)


def middle_kernel(*refs):
    parts = len(refs) // 3
    for kept, received, out in zip(refs[:parts], refs[parts : 2 * parts], refs[2 * parts :]):
        out[...] = (kept[0] + received[0].astype(jnp.float32)).astype(out.dtype)


def add_parts(refs, total):
    sides = len(refs) // 3
    part = total.shape[-1] // sides
    for side in range(sides):
        kept, first, last = refs[side::sides]
        rows = kept[0] + first[0].astype(jnp.float32) + last[...].astype(jnp.float32)
        total[:, :, side * part : side * part + part] = rows


def second_kernel(place_ref, *refs):
    add_parts(refs[:6], refs[-2])
    add_parts(refs[6:12], refs[-1])
    x_outs, y_outs = refs[12:14], refs[14:16]
    query_out, x_total, y_total = refs[16:]
    query_out[...] = y_total[:, NZ // 4 * NX * 16 :]

    def x_rows(out, chosen, side):
        for z in range(NZ // 4):
            rows = pl.ds(pl.multiple_of(chosen * 16, 16), 16)
            out[z] = side_of(x_total, z, rows, side, 1).astype(out.dtype)

    def y_rows(out, chosen, side):
        for z in range(NZ // 4):
            rows = pl.ds(pl.multiple_of(z * NX * 16 + chosen * 16, 16), 16)
            out[z] = side_of(y_total, 0, rows, side, 1).astype(out.dtype)

    split(place_ref, 4, x_rows, x_outs)
    split(place_ref, 0, y_rows, y_outs)


def last_kernel(*refs):
    out, x_total, y_total = refs[6:]
    half = x_total.shape[2]
    add_parts(refs[:3], x_total)
    add_parts(refs[3:6], y_total)
    out[:, :, :half] = x_total[...].astype(out.dtype)
    out[:, :, half:] = y_total[...].astype(out.dtype)


def encoded_kernel(order_ref, *refs):
    grads, pieces, out_ref, results, sems = refs[0], refs[1:-3], *refs[-3:]
    stores = []
    for k, piece in enumerate(pieces):
        total = dot_last(grads[0], piece[0]) + dot_last(grads[1], piece[1])
        results[k] = total.astype(jnp.bfloat16)
        columns = pl.ds(pl.multiple_of(order_ref[k] * 256, 256), 256)
        store = pltpu.make_async_copy(results.at[k], out_ref.at[:, columns], sems.at[k])
        store.start()
        stores.append(store)
    for store in stores:
        store.wait()


def kernel_call(kernel, name, out_shape, mebibytes=12, flops=0, moved=0, **options):
    return pl.pallas_call(
        kernel,
        out_shape=out_shape,
        compiler_params=pltpu.CompilerParams(vmem_limit_bytes=mebibytes * MIB),
        cost_estimate=pl.CostEstimate(flops=flops, bytes_accessed=moved, transcendentals=0),
        name=name,
        **options,
    )


def like(shape, dtype):
    return jax.ShapeDtypeStruct(shape, dtype)


def along(axis, step):
    def target(z, x, y, c):
        return (
            z + step * (axis == "z"),
            x + step * (axis == "x"),
            y + step * (axis == "y"),
            c + step * (axis == "core"),
        )

    return permutation(target)


def send(value, links):
    return lax.ppermute(value, AXES, links)


def tie(value, *after):
    return lax.optimization_barrier((value, *after))[0]


def flipped(axis, bits):
    return permutation(lambda z, x, y, c: (z, x ^ bits if axis == "x" else x, y ^ bits if axis == "y" else y, c))


def halving(outs, axes, steps, beside=()):
    kept, sent = outs[0::2], outs[1::2]
    sides = len(kept) // 2
    ways = [(axis, *bits) for axis in axes for bits in ((1, 3), (3, 1))[:sides]]
    first = [send(value, flipped(axis, near)) for value, (axis, near, _) in zip(sent, ways)]
    first = lax.optimization_barrier(first)

    def block(shape):
        return pl.BlockSpec((1, shape[1] // steps, *shape[2:]), lambda i: (1, i, 0, 0))

    shapes = [value.shape for value in kept]
    middle = kernel_call(
        middle_kernel,
        "middle",
        [like(shape[1:], jnp.bfloat16) for shape in shapes],
        grid=(steps,),
        in_specs=[block(shape) for shape in shapes] * 2,
        out_specs=[pl.BlockSpec((shape[1] // steps, *shape[2:]), lambda i: (i, 0, 0)) for shape in shapes],
    )(*kept, *first)
    last = [send(value, flipped(axis, far)) for value, (axis, _, far) in zip(middle, ways)]
    last, beside = lax.optimization_barrier((last, beside))
    operands, specs = [], []
    for start in (0, sides):
        for values in (kept, first, last):
            for value in values[start : start + sides]:
                operands.append(value)
                inner = value.shape[-3:]
                shape = (1,) * (value.ndim - 3) + (inner[0] // steps, *inner[1:])
                leading = (0,) * (value.ndim - 3)
                specs.append(pl.BlockSpec(shape, lambda i, leading=leading: (*leading, i, 0, 0)))
    return operands, specs, middle[0], beside


def on_device(queries, key_rows, value_rows, encoded, key_weight, value_weight, grad_out, lengths):
    _, answer, features = queries.shape
    keys = key_rows.shape[1]
    width = encoded.shape[2]
    pairs = features // PAIR
    half = features // 2
    dp, passage = lax.axis_index("dp").astype(jnp.int32), lax.axis_index("passage").astype(jnp.int32)
    x_place, y_place, core = dp % NX, passage // NC, passage % NC
    place = jnp.stack([p ^ bits for p in (x_place, y_place) for bits in range(4)])
    queries, grad_out = queries[0], grad_out[0]
    key_rows, value_rows, encoded = key_rows[0], value_rows[0], encoded[0]
    f32, bf16 = jnp.float32, jnp.bfloat16
    smem = pl.BlockSpec(memory_space=pltpu.SMEM)

    shard = jnp.stack([key_weight, value_weight])
    shards = [shard] + [send(shard, flipped("x", bits)) for bits in (1, 3)]

    stats_shape = like((3 * pairs, 2 * answer), f32)
    row_spec = pl.BlockSpec((answer, 2 * PAIR), lambda p: (0, p))
    key_spec = pl.BlockSpec((keys, 2 * PAIR), lambda p: (0, p))
    stats = kernel_call(
        stats_kernel,
        "stats",
        pltpu.VMEM(stats_shape.shape, f32),
        62,
        grid=(pairs // 2,),
        in_specs=[smem, row_spec, key_spec, key_spec, row_spec],
        out_specs=pl.BlockSpec(stats_shape.shape, lambda p: (0, 0)),
    )(lengths, queries, key_rows, value_rows, grad_out)

    stats = kernel_call(merge_kernel, "merge", stats_shape)(stats, send(stats, along("core", 1)))
    shards.append(send(tie(shards[1], stats), flipped("x", 3)))
    met, encoded_other = lax.optimization_barrier((send(stats, flipped("y", 1)), swap_cores(encoded)))
    stats = kernel_call(merge_kernel, "merge", stats_shape)(stats, met)
    all_stats = [stats, send(stats, flipped("y", 3))]

    def grads(first_pair, joint):
        def rows(p):
            return (0, first_pair // 2 + p)

        row_spec = pl.BlockSpec((answer, 2 * PAIR), rows)
        key_spec = pl.BlockSpec((keys, 2 * PAIR), rows)
        out_spec = pl.BlockSpec((keys, 2 * PAIR), lambda p: (0, p))
        stats_spec = pl.BlockSpec(stats_shape.shape, lambda p: (0, 0))
        query_spec = pl.BlockSpec((1, PAIR, answer), lambda p: (p, 0, 0))
        joint_spec = pl.BlockSpec((2, keys, 2 * PAIR), lambda p: (0, 0, first_pair // 2 + p))
        operands = (core[None], lengths, queries, key_rows, value_rows, grad_out, *all_stats)
        specs = [smem, smem, row_spec, key_spec, key_spec, row_spec] + [stats_spec] * len(all_stats)
        aliases = {}
        if joint is not None:
            aliases = {len(operands): 0}
            operands += (joint,)
            specs.append(pl.BlockSpec(memory_space=pl.ANY))
        return kernel_call(
            functools.partial(grads_kernel, first_pair),
            "grads",
            [
                pltpu.HBM((2, keys, features), bf16),
                like((keys, half), bf16),
                like((keys, half), bf16),
                like((NY // 2, PAIR, answer), f32),
                like((NY // 2, PAIR, answer), bf16),
            ],
            grid=(pairs // 4,),
            in_specs=specs,
            out_specs=[joint_spec, out_spec, out_spec, query_spec, query_spec],
            input_output_aliases=aliases,
        )(*operands)

    joint, mine_a, sent_a, query_kept_a, query_sent_a = grads(0, None)
    received_a = swap_cores(sent_a)

    whole_vmem = pl.BlockSpec(memory_space=pltpu.VMEM)
    shards = lax.optimization_barrier((*shards, mine_a))[:-1]
    ordered = kernel_call(
        arrange_kernel,
        "arrange",
        like((2, NX * shard.shape[1], features), bf16),
        in_specs=[smem] + [whole_vmem] * NX,
        out_specs=whole_vmem,
    )(place, *shards)

    around = permutation(lambda z, x, y, c: (z + 1 - 2 * c, x, y, c))
    pieces = [ordered, send(ordered, around)]

    joint, mine_b, sent_b, query_kept_b, query_sent_b = grads(pairs // 2, joint)
    received_b = swap_cores(sent_b)
    query_received = [swap_cores(query_sent_a), swap_cores(query_sent_b)]

    def blocks(shape):
        return pl.BlockSpec((shape[0] // 4, *shape[1:]), lambda i: (i, 0, 0))

    whole = pl.BlockSpec((keys, half), lambda i: (0, 0))
    encoded_spec = pl.BlockSpec((keys, width // 4), lambda i: (0, i))
    query_spec = pl.BlockSpec(query_kept_a.shape, lambda i: (0, 0, 0))
    query_rows = PAIR * answer // half // 4
    x_shape = (2, NZ, 64, half // 2)
    y_shape = (2, 4, NZ // 4 * NX * 16 + query_rows, half // 2)

    def split_outs(shape, sides):
        spec = pl.BlockSpec((2, shape[1] // 4, *shape[2:]), lambda i: (0, i, 0, 0))
        return [like(shape, f32), like(shape, bf16)] * sides, [spec] * 2 * sides

    def total(shape):
        return pltpu.VMEM((shape[1] // 4, shape[2], 2 * shape[3]), f32)

    x_outs, x_specs = split_outs(x_shape, 2)
    y_outs, y_specs = split_outs(y_shape, 2)
    terms = kernel_call(
        weights_kernel,
        "weights",
        x_outs + y_outs,
        20,
        grid=(4,),
        in_specs=[smem, encoded_spec, encoded_spec] + [whole] * 4 + [query_spec] * 4,
        out_specs=x_specs + y_specs,
        scratch_shapes=[pltpu.VMEM((1, width // 4, half), f32)] * 2
        + [pltpu.VMEM((NY, 2, query_rows, answer), f32)],
    )(
        place,
        encoded,
        encoded_other,
        mine_a,
        mine_b,
        received_a,
        received_b,
        query_kept_a,
        query_kept_b,
        *query_received,
    )

    pieces.append(send(tie(pieces[1], terms[0]), around))

    operands, specs, middle, _ = halving(terms, "xy", 4)
    pieces.append(send(tie(pieces[2], middle), around))
    chunk, query_shape = (2, NZ, 16, half), (4, query_rows, half)
    chunk_outs, chunk_specs = split_outs(chunk, 1)
    *second, query_grad = kernel_call(
        second_kernel,
        "second",
        chunk_outs * 2 + [like(query_shape, f32)],
        grid=(4,),
        in_specs=[smem] + specs,
        out_specs=chunk_specs * 2 + [blocks(query_shape)],
        scratch_shapes=[total(x_shape), total(y_shape)],
    )(place, *operands)
    query_grad = query_grad.reshape(4, query_rows, 2, answer).transpose(2, 0, 1, 3)
    query_grad = query_grad.reshape(PAIR, answer).T.astype(bf16)[None]

    across = send(tie(pieces[3], second[0]), around)
    operands, specs, _, across = halving(second, "yx", 1, across)
    last = kernel_call(
        last_kernel,
        "last",
        like((NZ, 16, features), bf16),
        grid=(1,),
        in_specs=specs,
        out_specs=pl.BlockSpec((NZ, 16, features), lambda i: (0, 0, 0)),
        scratch_shapes=[pltpu.VMEM((NZ, 16, half), f32)] * 2,
    )(*operands)
    swapped = [swap_cores(tie(piece, last)) for piece in pieces[1:4]]
    last = lax.all_to_all(
        last.reshape(NZ * NC, 8, features),
        AXES,
        0,
        0,
        tiled=True,
        axis_index_groups=groups(lambda z, x, y, c: (x, y)),
    )

    z_place, way = dp // NX, 1 - 2 * core
    order = [(z_place + way * step + NZ) % NZ for step in (0, -1, -2, -3, 1, 2, 3, 4)]
    in_hbm = pl.BlockSpec(memory_space=pltpu.HBM)
    encoded_grad = kernel_call(
        encoded_kernel,
        "encoded",
        pltpu.HBM((keys, width), bf16),
        24,
        flops=4 * keys * width * features,
        moved=14 * MIB,
        in_specs=[smem] + [whole_vmem] * (NZ + 1),
        out_specs=in_hbm,
        scratch_shapes=[
            pltpu.VMEM((NZ, keys, width // NZ), bf16),
            pltpu.SemaphoreType.DMA((NZ,)),
        ],
    )(jnp.stack(order), joint, *pieces, *swapped, across)
    summed = tie(last, encoded_grad).reshape(NZ, NC, 8, features).astype(f32).sum(0)
    key_weight_grad, value_weight_grad = summed[0], summed[1]
    return query_grad, encoded_grad[None], key_weight_grad, value_weight_grad


def solution(mesh):
    return jax.shard_map(
        on_device,
        mesh=mesh,
        in_specs=(
            P("dp", None, None),
            P("dp", "passage", None),
            P("dp", "passage", None),
            P("dp", "passage", None),
            P("dp", None),
            P("dp", None),
            P("dp", None, None),
            P("dp"),
        ),
        out_specs=(
            P("dp", None, "passage"),
            P("dp", "passage", None),
            P(("dp", "passage"), None),
            P(("dp", "passage"), None),
        ),
        check_vma=False,
    )
```
